32 devices in a mesh: grp: 2 (over x), blk: 16 (over z, y, core).
Axes of the slice: x: 2, y: 2, z: 4, core: 2. Of those that a mesh axis runs over, the one named last changes fastest.
Arguments:
- tokens: bfloat16 [4096, 1152], P(('grp', 'blk')), may hold values from -6 to 6
- segment_ids: int32 [4096], P(('grp', 'blk')), may hold values from 0 to 3, as said below
- ln1_gain: float32 [1152], replicated, may hold values from 0.5 to 1.5
- ln1_bias: float32 [1152], replicated, may hold values from -4 to 4
- qkv_weight: bfloat16 [1152, 3456], P('blk'), may hold values from -0.1875 to 0.1875
- q_bias: float32 [1152], replicated, may hold values from -4 to 4
- v_bias: float32 [1152], replicated, may hold values from -0.8 to 0.8
- out_weight: bfloat16 [1152, 1152], P('blk'), may hold values from -1.5 to 1.5
- out_bias: float32 [1152], replicated, may hold values from -2.4 to 2.4
- ln2_gain: float32 [1152], replicated, may hold values from 0.5 to 1.5
- ln2_bias: float32 [1152], replicated, may hold values from -4 to 4
- fc1_weight: bfloat16 [1152, 4304], P('blk'), may hold values from -0.1875 to 0.1875
- fc1_bias: float32 [4304], replicated, may hold values from -4 to 4
- fc2_weight: bfloat16 [1152, 4304], P('blk'), may hold values from -0.09375 to 0.09375
- fc2_bias: float32 [1152], replicated, may hold values from -2.4 to 2.4
- bridge_gate: bfloat16 [1152, 14336], P(None, 'blk'), may hold values from -0.1875 to 0.1875
- bridge_up: bfloat16 [1152, 14336], P(None, 'blk'), may hold values from -0.1875 to 0.1875
- bridge_down: bfloat16 [14336, 4096], P('blk'), may hold values from -0.046875 to 0.046875
- context_gain: float32 [4096], replicated, may hold values from 0.5 to 1.5
- latents: bfloat16 [64, 4096], replicated, may hold values from -6 to 6
- latent_gain: float32 [4096], replicated, may hold values from 0.5 to 1.5
- query_weight: bfloat16 [4096, 1536], P('blk'), may hold values from -0.09375 to 0.09375
- key_weight: bfloat16 [4096, 384], P('blk'), may hold values from -0.09375 to 0.09375
- value_weight: bfloat16 [4096, 384], P('blk'), may hold values from -0.09375 to 0.09375
- mixer_weight: bfloat16 [1536, 4096], P('blk'), may hold values from -0.875 to 0.875
- post_gain: float32 [4096], replicated, may hold values from 0.5 to 1.5
- latent_gate: bfloat16 [4096, 16384], P(None, 'blk'), may hold values from -0.09375 to 0.09375
- latent_up: bfloat16 [4096, 16384], P(None, 'blk'), may hold values from -0.09375 to 0.09375
- latent_down: bfloat16 [16384, 4096], P('blk'), may hold values from -0.046875 to 0.046875
- cotangent: bfloat16 [512, 4096], P('grp'), may hold values from -6 to 6
Outputs:
- latents_out: bfloat16 [512, 4096], P(('grp', 'blk'))
- grad_tokens: float32 [4096, 1152], P(('grp', 'blk'))
- grad_ln1_gain: float32 [1152], replicated
- grad_ln1_bias: float32 [1152], replicated
- grad_qkv_weight: float32 [1152, 3456], P(('grp', 'blk'))
- grad_q_bias: float32 [1152], replicated
- grad_v_bias: float32 [1152], replicated
- grad_out_weight: float32 [1152, 1152], P(('grp', 'blk'))
- grad_out_bias: float32 [1152], replicated
- grad_ln2_gain: float32 [1152], replicated
- grad_ln2_bias: float32 [1152], replicated
- grad_fc1_weight: float32 [1152, 4304], P(('grp', 'blk'))
- grad_fc1_bias: float32 [4304], replicated
- grad_fc2_weight: float32 [1152, 4304], P(('grp', 'blk'))
- grad_fc2_bias: float32 [1152], replicated
- grad_bridge_gate: float32 [1152, 14336], P(None, 'blk')
- grad_bridge_up: float32 [1152, 14336], P(None, 'blk')
- grad_bridge_down: float32 [14336, 4096], P('blk')
- grad_context_gain: float32 [4096], replicated
- grad_latents: float32 [64, 4096], replicated
- grad_latent_gain: float32 [4096], replicated
- grad_query_weight: float32 [4096, 1536], P(('grp', 'blk'))
- grad_key_weight: float32 [4096, 384], P(('grp', 'blk'))
- grad_value_weight: float32 [4096, 384], P(('grp', 'blk'))
- grad_mixer_weight: float32 [1536, 4096], P(('grp', 'blk'))
- grad_post_gain: float32 [4096], replicated
- grad_latent_gate: float32 [4096, 16384], P(None, 'blk')
- grad_latent_up: float32 [4096, 16384], P(None, 'blk')
- grad_latent_down: float32 [16384, 4096], P('blk')
The draws below stay inside these ranges and needn't reach their ends.
Inputs may be any that keep to these rules, and one draw needn't show every extreme that they name: `segment_ids`: patches of one pack with equal ids belong to one image; ids are only compared within a pack. Each pack holds 4 images, each of one patch or more, at most 1024 patches each and one of exactly 1024. A pack is cut into blocks of 64 consecutive patches, placed on the pack's devices in a drawn order, two blocks a device, so the patches of one image may lie on many devices; in every pack some image has patches on the first and on the last device of blk.
All inputs are finite; a program needn't handle non-finite values.
Results may differ from the reference program's by a relative error of at most 0.028.
Values may be sent and summed in bfloat16 or wider, within the bound.
No kernel may reach another device: no remote copies, remote signals or barrier semaphores. Data moves between devices by JAX's collectives and lax.ppermute only.
A program may use at most 576 MiB of HBM per device.

```python
import jax
import jax.numpy as jnp
from jax import lax

D = 1152
HEADS = 16
HEAD = 72
FF = 4304
BRIDGE = 14336
MODEL = 4096
LATENTS = 64
P_HEADS = 16
P_KV = 4
P_HEAD = 96
P_FF = 16384
TOK_DEV = 128
TOKENS = 4096
PATCH_MOST = 1024
IMAGES = 4
LAT_ROWS = 256
N_GRP = 2
N_BLK = 16


def image_group(key):
    group_rows = TOK_DEV * N_BLK
    half = TOK_DEV // 2
    pieces = 2 * N_BLK
    rest_count = IMAGES - 1
    rest_rows = group_rows - PATCH_MOST
    key_lengths, key_order = jax.random.split(key)
    shares = jax.random.randint(key_lengths, (rest_count,), 2, 4, dtype=jnp.int32)
    parts = rest_rows * shares // jnp.sum(shares)
    parts = parts.at[rest_count - 1].add(rest_rows - jnp.sum(parts))
    lengths = jnp.concatenate([jnp.full((1,), PATCH_MOST, jnp.int32), parts])
    bounds = jnp.cumsum(lengths)[:rest_count]
    position = jnp.arange(group_rows, dtype=jnp.int32)
    labels = jnp.sum((position[:, None] >= bounds[None, :]).astype(jnp.int32), axis=1)
    middle = 2 + jax.random.permutation(key_order, pieces - 2).astype(jnp.int32)
    order = jnp.concatenate([jnp.zeros((1,), jnp.int32), middle, jnp.ones((1,), jnp.int32)])
    return labels.reshape(pieces, half)[order].reshape(group_rows)


def draw_segment_ids(key, part):
    key = jax.random.fold_in(key, 5)
    return jnp.concatenate([image_group(jax.random.fold_in(key, index)) for index in range(N_GRP)])


def levels(stream_key, shape, cuts, least, largest):
    def one(dim, shards_of):
        draws = jax.random.uniform(jax.random.fold_in(jax.random.fold_in(stream_key, 6), dim), (shards_of,), jnp.float32, least / len(cuts), largest / len(cuts))
        return jnp.repeat(jnp.exp(draws), shape[dim] // shards_of).reshape((-1,) + (1,) * (len(shape) - dim - 1))

    level = one(*cuts[0])
    for cut in cuts[1:]:
        level = level * one(*cut)
    return level


def normal_values(rng, shape, scale, reach, cuts=(), held_as=jnp.bfloat16):
    values = jax.random.normal(rng, shape, jnp.float32) * scale
    if len(cuts) > 0:
        values = levels(rng, shape, cuts, -0.22, 0.18) * values
    return jnp.clip(values, min=-reach, max=reach).astype(held_as)


def setup_inputs(seed: int = 0) -> dict:
    key_list = jax.random.split(jax.random.key(seed), 31)
    tokens = normal_values(key_list[0], (TOKENS, D), 1.0, 6.0, ((0, 32),))
    segment_ids = draw_segment_ids(jax.random.fold_in(key_list[30], 71), 0)
    ln1_gain = jnp.clip(1.0 + 0.1 * jax.random.normal(key_list[2], (D,), jnp.float32), 0.5, 1.5)
    ln1_bias = normal_values(key_list[3], (D,), 0.5, 4.0, (), jnp.float32)
    qkv_weight = normal_values(key_list[4], (D, 3 * D), D ** -0.5, 0.1875, ((0, 16),))
    q_bias = normal_values(key_list[5], (D,), 0.5, 4.0, (), jnp.float32)
    v_bias = normal_values(key_list[6], (D,), 0.1, 0.8, (), jnp.float32)
    out_weight = normal_values(key_list[7], (D, D), (D // 64) ** -0.5, 1.5, ((0, 16),))
    out_bias = normal_values(key_list[8], (D,), 0.3, 2.4, (), jnp.float32)
    ln2_gain = jnp.clip(1.0 + 0.1 * jax.random.normal(key_list[9], (D,), jnp.float32), 0.5, 1.5)
    ln2_bias = normal_values(key_list[10], (D,), 0.5, 4.0, (), jnp.float32)
    fc1_weight = normal_values(key_list[11], (D, FF), D ** -0.5, 0.1875, ((0, 16),))
    fc1_bias = normal_values(key_list[12], (FF,), 0.5, 4.0, (), jnp.float32)
    fc2_weight = normal_values(key_list[13], (D, FF), FF ** -0.5, 0.09375, ((0, 16),))
    fc2_bias = normal_values(key_list[14], (D,), 0.3, 2.4, (), jnp.float32)
    bridge_gate = normal_values(key_list[15], (D, BRIDGE), D ** -0.5, 0.1875, ((1, 16),))
    bridge_up = normal_values(key_list[16], (D, BRIDGE), D ** -0.5, 0.1875, ((1, 16),))
    bridge_down = normal_values(key_list[17], (BRIDGE, MODEL), BRIDGE ** -0.5, 0.046875, ((0, 16),))
    context_gain = jnp.clip(1.0 + 0.1 * jax.random.normal(key_list[18], (MODEL,), jnp.float32), 0.5, 1.5)
    latents = normal_values(key_list[19], (LATENTS, MODEL), 1.0, 6.0)
    latent_gain = jnp.clip(1.0 + 0.1 * jax.random.normal(key_list[20], (MODEL,), jnp.float32), 0.5, 1.5)
    query_weight = normal_values(key_list[21], (MODEL, P_HEADS * P_HEAD), MODEL ** -0.5, 0.09375, ((0, 16),))
    key_weight = normal_values(key_list[22], (MODEL, P_KV * P_HEAD), MODEL ** -0.5, 0.09375, ((0, 16),))
    value_weight = normal_values(key_list[23], (MODEL, P_KV * P_HEAD), MODEL ** -0.5, 0.09375, ((0, 16),))
    mixer_weight = normal_values(key_list[24], (P_HEADS * P_HEAD, MODEL), (P_HEADS * P_HEAD // 32) ** -0.5, 0.875, ((0, 16),))
    post_gain = jnp.clip(1.0 + 0.1 * jax.random.normal(key_list[25], (MODEL,), jnp.float32), 0.5, 1.5)
    latent_gate = normal_values(key_list[26], (MODEL, P_FF), MODEL ** -0.5, 0.09375, ((1, 16),))
    latent_up = normal_values(key_list[27], (MODEL, P_FF), MODEL ** -0.5, 0.09375, ((1, 16),))
    latent_down = normal_values(key_list[28], (P_FF, MODEL), P_FF ** -0.5, 0.046875, ((0, 16),))
    cotangent = normal_values(key_list[29], (N_GRP * LAT_ROWS, MODEL), 1.0, 6.0, ((0, 2),))
    return {"tokens": tokens, "segment_ids": segment_ids, "ln1_gain": ln1_gain, "ln1_bias": ln1_bias, "qkv_weight": qkv_weight, "q_bias": q_bias, "v_bias": v_bias, "out_weight": out_weight, "out_bias": out_bias, "ln2_gain": ln2_gain, "ln2_bias": ln2_bias, "fc1_weight": fc1_weight, "fc1_bias": fc1_bias, "fc2_weight": fc2_weight, "fc2_bias": fc2_bias, "bridge_gate": bridge_gate, "bridge_up": bridge_up, "bridge_down": bridge_down, "context_gain": context_gain, "latents": latents, "latent_gain": latent_gain, "query_weight": query_weight, "key_weight": key_weight, "value_weight": value_weight, "mixer_weight": mixer_weight, "post_gain": post_gain, "latent_gate": latent_gate, "latent_up": latent_up, "latent_down": latent_down, "cotangent": cotangent}


@jax.custom_vjp
def low(v):
    return lax.optimization_barrier(v.astype(jnp.bfloat16)).astype(jnp.float32)

@jax.custom_vjp
def low_back(v):
    return v

def low_keep(v):
    return (low(v), None)

def low_pass(kept, grad):
    return (grad,)

def back_keep(v):
    return (v, None)

def back_low(kept, grad):
    return (low(grad),)
low.defvjp(low_keep, low_pass)
low_back.defvjp(back_keep, back_low)
highest = lax.Precision.HIGHEST
norm_eps = 1e-06
masked_score = -1e+30

def layer_norm(values, gain, bias):
    center = values - lax.optimization_barrier(jnp.mean(values, axis=-1, keepdims=True))
    spread = lax.optimization_barrier(jnp.mean(center * center, axis=-1, keepdims=True))
    return center * lax.rsqrt(spread + norm_eps) * gain + bias

def rms_norm(values, gain):
    return values * lax.rsqrt(lax.optimization_barrier(jnp.mean(values * values, axis=-1, keepdims=True)) + norm_eps) * gain

def swiglu(gate, up):
    return jax.nn.silu(gate) * up

def matmul(left, right):
    return jnp.dot(left, right, precision=highest)

def attend(queries, keys, values, image_ids):
    rows = queries.shape[0]
    features = queries.shape[1]
    width = 512 if rows % 512 == 0 else rows
    key_heads = keys.reshape(rows, HEADS, HEAD)
    value_heads = values.reshape(rows, HEADS, HEAD)

    def block(pair):
        query_rows, query_ids = pair
        scores = jnp.einsum('thd,shd->hts', query_rows.reshape(width, HEADS, HEAD), key_heads, precision=highest) * HEAD ** (-0.5)
        scores = low_back(scores)
        mask = (query_ids[:, None] == image_ids[None, :])[None]
        scores = jnp.where(mask, scores, masked_score)
        top = lax.optimization_barrier(jnp.max(scores, axis=-1, keepdims=True))
        lse = top + jnp.log(lax.optimization_barrier(jnp.sum(jnp.exp(scores - top), axis=-1, keepdims=True)))
        probs = low(jnp.exp(scores - lse))
        mixed = jnp.einsum('hts,shd->thd', probs, value_heads, precision=highest)
        return mixed.reshape(width, features)
    blocks = lax.map(jax.checkpoint(block), (queries.reshape(rows // width, width, features), image_ids.reshape(rows // width, width)))
    return blocks.reshape(rows, features)

def resample(latent_queries, latent_keys, latent_values, patch_keys, patch_values, image_ids):
    groups = P_HEADS // P_KV
    scale = P_HEAD ** (-0.5)
    query_heads = latent_queries.reshape(LATENTS, P_KV, groups, P_HEAD)
    patch_key_heads = patch_keys.reshape(patch_keys.shape[0], P_KV, P_HEAD)
    patch_value_heads = patch_values.reshape(patch_values.shape[0], P_KV, P_HEAD)
    latent_key_heads = latent_keys.reshape(LATENTS, P_KV, P_HEAD)
    latent_value_heads = latent_values.reshape(LATENTS, P_KV, P_HEAD)

    def one_image(image):
        mask = (image_ids == image)[None, None, None, :]
        patch_scores = low_back(jnp.einsum('lgrd,tgd->grlt', query_heads, patch_key_heads, precision=highest) * scale)
        latent_scores = low_back(jnp.einsum('lgrd,kgd->grlk', query_heads, latent_key_heads, precision=highest) * scale)
        patch_scores = jnp.where(mask, patch_scores, masked_score)
        top = jnp.maximum(lax.optimization_barrier(jnp.max(patch_scores, axis=-1, keepdims=True)), lax.optimization_barrier(jnp.max(latent_scores, axis=-1, keepdims=True)))
        total = lax.optimization_barrier(jnp.sum(jnp.exp(patch_scores - top), axis=-1, keepdims=True)) + lax.optimization_barrier(jnp.sum(jnp.exp(latent_scores - top), axis=-1, keepdims=True))
        lse = top + jnp.log(total)
        patch_probs = low(jnp.exp(patch_scores - lse))
        latent_probs = low(jnp.exp(latent_scores - lse))
        mixed = jnp.einsum('grlt,tgd->lgrd', patch_probs, patch_value_heads, precision=highest)
        mixed = mixed + jnp.einsum('grlk,kgd->lgrd', latent_probs, latent_value_heads, precision=highest)
        return mixed.reshape(LATENTS, P_HEADS * P_HEAD)
    images = lax.map(jax.checkpoint(one_image), jnp.arange(IMAGES, dtype=jnp.int32))
    return images.reshape(IMAGES * LATENTS, P_HEADS * P_HEAD)

def reference(tokens, segment_ids, ln1_gain, ln1_bias, qkv_weight, q_bias, v_bias, out_weight, out_bias, ln2_gain, ln2_bias, fc1_weight, fc1_bias, fc2_weight, fc2_bias, bridge_gate, bridge_up, bridge_down, context_gain, latents, latent_gain, query_weight, key_weight, value_weight, mixer_weight, post_gain, latent_gate, latent_up, latent_down, cotangent):
    group_rows = TOK_DEV * N_BLK

    def forward(inputs, ln1_gain, ln1_bias, qkv_weight, q_bias, v_bias, out_weight, out_bias, ln2_gain, ln2_bias, fc1_weight, fc1_bias, fc2_weight, fc2_bias, bridge_gate, bridge_up, bridge_down, context_gain, latents, latent_gain, query_weight, key_weight, value_weight, mixer_weight, post_gain, latent_gate, latent_up, latent_down):
        features = inputs.shape[1]
        first_in = low(layer_norm(inputs, ln1_gain, ln1_bias))
        projected = matmul(first_in, qkv_weight)
        queries = low_back(low(projected[:, :features] + q_bias))
        keys = low_back(low(projected[:, features:2 * features]))
        values = low_back(low(projected[:, 2 * features:] + v_bias))
        packs = []
        for index in range(N_GRP):
            first = index * group_rows
            last = first + group_rows
            packs.append(attend(queries[first:last], keys[first:last], values[first:last], segment_ids[first:last]))
        attended = low_back(low(jnp.concatenate(packs, axis=0)))
        hidden_state = inputs + low_back(matmul(attended, out_weight)) + out_bias
        second_in = low(layer_norm(hidden_state, ln2_gain, ln2_bias))
        pre = low_back(matmul(second_in, fc1_weight) + fc1_bias)
        act = low(jax.nn.gelu(pre, approximate=True))
        encoded = hidden_state + low_back(matmul(act, fc2_weight.T)) + fc2_bias
        bridge_in = low(encoded)
        gate_pre = low_back(matmul(bridge_in, bridge_gate))
        up_pre = low_back(matmul(bridge_in, bridge_up))
        context = low_back(matmul(low(swiglu(gate_pre, up_pre)), bridge_down))
        context_in = low(rms_norm(context, context_gain))
        latent_in = low(rms_norm(latents, latent_gain))
        latent_queries = low_back(low(matmul(latent_in, query_weight)))
        latent_keys = low_back(low(matmul(latent_in, key_weight)))
        latent_values = low_back(low(matmul(latent_in, value_weight)))
        patch_keys = low_back(low(matmul(context_in, key_weight)))
        patch_values = low_back(low(matmul(context_in, value_weight)))
        resampled = []
        for index in range(N_GRP):
            first = index * group_rows
            last = first + group_rows
            resampled.append(resample(latent_queries, latent_keys, latent_values, patch_keys[first:last], patch_values[first:last], segment_ids[first:last]))
        attended_latent = low_back(low(jnp.concatenate(resampled, axis=0)))
        latent_state = jnp.tile(latents, (N_GRP * IMAGES, 1)) + low_back(matmul(attended_latent, mixer_weight))
        post_in = low(rms_norm(latent_state, post_gain))
        latent_gate_pre = low_back(matmul(post_in, latent_gate))
        latent_up_pre = low_back(matmul(post_in, latent_up))
        return latent_state + matmul(low(swiglu(latent_gate_pre, latent_up_pre)), latent_down)
    result, pullback = jax.vjp(forward, tokens.astype(jnp.float32), ln1_gain.astype(jnp.float32), ln1_bias.astype(jnp.float32), qkv_weight.astype(jnp.float32), q_bias.astype(jnp.float32), v_bias.astype(jnp.float32), out_weight.astype(jnp.float32), out_bias.astype(jnp.float32), ln2_gain.astype(jnp.float32), ln2_bias.astype(jnp.float32), fc1_weight.astype(jnp.float32), fc1_bias.astype(jnp.float32), fc2_weight.astype(jnp.float32), fc2_bias.astype(jnp.float32), bridge_gate.astype(jnp.float32), bridge_up.astype(jnp.float32), bridge_down.astype(jnp.float32), context_gain.astype(jnp.float32), latents.astype(jnp.float32), latent_gain.astype(jnp.float32), query_weight.astype(jnp.float32), key_weight.astype(jnp.float32), value_weight.astype(jnp.float32), mixer_weight.astype(jnp.float32), post_gain.astype(jnp.float32), latent_gate.astype(jnp.float32), latent_up.astype(jnp.float32), latent_down.astype(jnp.float32))
    grads = pullback(cotangent.astype(jnp.float32))
    return (result.astype(jnp.bfloat16), grads[0], grads[1], grads[2], grads[3], grads[4], grads[5], grads[6], grads[7], grads[8], grads[9], grads[10], grads[11], grads[12], grads[13], grads[14], grads[15], grads[16], grads[17], grads[18], grads[19], grads[20], grads[21], grads[22], grads[23], grads[24], grads[25], grads[26], grads[27])
```

```python
import functools

import jax
import jax.numpy as jnp
from jax import lax
from jax.experimental import pallas as pl
from jax.experimental.pallas import tpu as pltpu
from jax.sharding import PartitionSpec as P

HEADS = 16
HEAD = 72
LATENTS = 64
P_HEADS = 16
P_KV = 4
P_HEAD = 96
LANES = 128

masked_score = -1e30
norm_eps = 1e-06
vmem_bytes = 56 * 2**20
low = jnp.bfloat16
wide = jnp.float32


def layer_norm(values, gain, bias):
    center = values - jnp.mean(values, axis=-1, keepdims=True)
    spread = jnp.mean(center * center, axis=-1, keepdims=True)
    return center * lax.rsqrt(spread + norm_eps) * gain + bias


def rms_norm(values, gain):
    return values * lax.rsqrt(jnp.mean(values * values, axis=-1, keepdims=True) + norm_eps) * gain


def smooth_gate(values):
    return jax.nn.gelu(values, approximate=True)


def swiglu(gate, up):
    return jax.nn.silu(gate) * up


def mat_times(left, right):
    return jnp.dot(left, right, preferred_element_type=wide)


def contract(left, right, left_dim, right_dim):
    return lax.dot_general(
        left, right, (((left_dim,), (right_dim,)), ((), ())), preferred_element_type=wide
    )


def mat_times_t(left, right):
    return contract(left, right, 1, 1)


def outer_sum(left, right):
    return contract(left, right, 0, 0)


def rows_at(array, first, width, axis=0):
    return lax.dynamic_slice_in_dim(array, first, width, axis)


def gather(array):
    return lax.all_gather(array, "blk", axis=0, tiled=True)


def scatter_sum(array):
    return lax.psum_scatter(array.astype(low), "blk", scatter_dimension=0, tiled=True).astype(wide)


def swap_pieces(pieces):
    flat = pieces.reshape((-1,) + pieces.shape[2:])
    return lax.all_to_all(flat, "blk", 0, 0, tiled=True)


def attend_kernel(query_ref, key_ref, value_ref, row_ids_ref, col_ids_ref, out_ref):
    scores = mat_times_t(query_ref[...], key_ref[...]) * HEAD ** (-0.5)
    mask = row_ids_ref[...] == col_ids_ref[...]
    scores = jnp.where(mask, scores, masked_score)
    top = jnp.max(scores, axis=-1, keepdims=True)
    weights = jnp.exp(scores - top)
    total = jnp.sum(weights, axis=-1, keepdims=True)
    probs = (weights * (1.0 / total)).astype(low)
    out_ref[...] = mat_times(probs, value_ref[...]).astype(low)


def query_rows_for(rows):
    return 256 if rows <= 2048 else 64


def attend(heads, row_ids, col_ids):
    rows = heads.shape[0]
    width = query_rows_for(rows)
    return pl.pallas_call(
        attend_kernel,
        out_shape=jax.ShapeDtypeStruct((rows, LANES), low),
        grid=(rows // width,),
        in_specs=[
            pl.BlockSpec((width, LANES), lambda i: (i, 0)),
            pl.BlockSpec((rows, LANES), lambda i: (0, 1)),
            pl.BlockSpec((rows, LANES), lambda i: (0, 2)),
            pl.BlockSpec((width, 1), lambda i: (i, 0)),
            pl.BlockSpec((1, rows), lambda i: (0, 0)),
        ],
        out_specs=pl.BlockSpec((width, LANES), lambda i: (i, 0)),
        compiler_params=pltpu.CompilerParams(vmem_limit_bytes=vmem_bytes),
        name="vision_attend",
    )(heads, heads, heads, row_ids, col_ids)


def attend_back_kernel(
    query_ref, key_ref, value_ref, grad_ref, row_ids_ref, col_ids_ref,
    query_grad_ref, key_grad_ref, value_grad_ref, key_sum, value_sum,
):
    step = pl.program_id(0)

    @pl.when(step == 0)
    def _():
        key_sum[...] = jnp.zeros_like(key_sum)
        value_sum[...] = jnp.zeros_like(value_sum)

    queries = query_ref[...]
    grads = grad_ref[...]
    scores = mat_times_t(key_ref[...], queries) * HEAD ** (-0.5)
    mask = row_ids_ref[...] == col_ids_ref[...]
    scores = jnp.where(mask, scores, masked_score)
    top = jnp.max(scores, axis=0, keepdims=True)
    weights = jnp.exp(scores - top)
    total = jnp.sum(weights, axis=0, keepdims=True)
    probs = weights * (1.0 / total)
    dprob = mat_times_t(value_ref[...], grads)
    delta = jnp.sum(probs * dprob, axis=0, keepdims=True)
    score_grad = (probs * (dprob - delta)).astype(low)
    key_sum[...] += mat_times(score_grad, queries)
    value_sum[...] += mat_times(probs.astype(low), grads)
    query_grad_ref[...] = (outer_sum(score_grad, key_ref[...]) * HEAD ** (-0.5)).astype(low)

    @pl.when(step == pl.num_programs(0) - 1)
    def _():
        key_grad_ref[...] = (key_sum[...] * HEAD ** (-0.5)).astype(low)
        value_grad_ref[...] = value_sum[...].astype(low)


def attend_back(heads, grads, row_ids, col_ids):
    rows = heads.shape[0]
    width = query_rows_for(rows)
    return pl.pallas_call(
        attend_back_kernel,
        out_shape=[jax.ShapeDtypeStruct((rows, LANES), low)] * 3,
        grid=(rows // width,),
        in_specs=[
            pl.BlockSpec((width, LANES), lambda i: (i, 0)),
            pl.BlockSpec((rows, LANES), lambda i: (0, 1)),
            pl.BlockSpec((rows, LANES), lambda i: (0, 2)),
            pl.BlockSpec((width, LANES), lambda i: (i, 0)),
            pl.BlockSpec((rows, 1), lambda i: (0, 0)),
            pl.BlockSpec((1, width), lambda i: (0, i)) if width % LANES == 0
            else pl.BlockSpec((None, 1, width), lambda i: (i, 0, 0)),
        ],
        out_specs=[
            pl.BlockSpec((width, LANES), lambda i: (i, 0)),
            pl.BlockSpec((rows, LANES), lambda i: (0, 0)),
            pl.BlockSpec((rows, LANES), lambda i: (0, 0)),
        ],
        scratch_shapes=[pltpu.VMEM((rows, LANES), wide)] * 2,
        compiler_params=pltpu.CompilerParams(vmem_limit_bytes=vmem_bytes),
        name="vision_attend_back",
    )(
        heads, heads, heads, grads, row_ids,
        col_ids if width % LANES == 0 else col_ids.reshape(rows // width, 1, width),
    )


def image_probs(scores, self_scores, mask):
    scores = jnp.where(mask, scores, masked_score)
    top = jnp.maximum(
        jnp.max(scores, axis=-1, keepdims=True), jnp.max(self_scores, axis=-1, keepdims=True)
    )
    weights = jnp.where(mask, jnp.exp(scores - top), 0.0)
    self_weights = jnp.exp(self_scores - top)
    total = jnp.sum(weights, axis=-1, keepdims=True) + jnp.sum(
        self_weights, axis=-1, keepdims=True
    )
    scale = 1.0 / total
    return weights * scale, self_weights * scale


def resample_kernel(
    query_ref, key_ref, value_ref, self_key_ref, self_value_ref, ids_ref, out_ref, *, images
):
    queries = query_ref[...]
    scores = mat_times_t(queries, key_ref[...]) * P_HEAD ** (-0.5)
    self_scores = mat_times_t(queries, self_key_ref[...]) * P_HEAD ** (-0.5)
    for image in range(images):
        probs, self_probs = image_probs(scores, self_scores, ids_ref[...] == image)
        mixed = mat_times(probs.astype(low), value_ref[...])
        mixed += mat_times(self_probs.astype(low), self_value_ref[...])
        out_ref[pl.ds(image * LATENTS, LATENTS), :] = mixed.astype(low)


def resample(queries, keys, values, self_keys, self_values, ids, images):
    return pl.pallas_call(
        functools.partial(resample_kernel, images=images),
        out_shape=jax.ShapeDtypeStruct((images * LATENTS, LANES), low),
        compiler_params=pltpu.CompilerParams(vmem_limit_bytes=vmem_bytes),
        name="resampler_attend",
    )(queries, keys, values, self_keys, self_values, ids)


def resample_back_kernel(
    query_ref, key_ref, value_ref, self_key_ref, self_value_ref, ids_ref, grad_ref,
    query_grad_ref, key_grad_ref, value_grad_ref, self_key_grad_ref, self_value_grad_ref,
    *, images,
):
    queries = query_ref[...]
    scale = P_HEAD ** (-0.5)
    scores = mat_times_t(queries, key_ref[...]) * scale
    self_scores = mat_times_t(queries, self_key_ref[...]) * scale
    for image in range(images):
        probs, self_probs = image_probs(scores, self_scores, ids_ref[...] == image)
        grads = grad_ref[pl.ds(image * LATENTS, LATENTS), :]
        dprob = mat_times_t(grads, value_ref[...])
        self_dprob = mat_times_t(grads, self_value_ref[...])
        delta = jnp.sum(probs * dprob, axis=-1, keepdims=True) + jnp.sum(
            self_probs * self_dprob, axis=-1, keepdims=True
        )
        score_grad = (probs * (dprob - delta)).astype(low)
        self_score_grad = (self_probs * (self_dprob - delta)).astype(low)
        terms = (
            mat_times(score_grad, key_ref[...]) + mat_times(self_score_grad, self_key_ref[...]),
            outer_sum(score_grad, queries),
            outer_sum(probs.astype(low), grads),
            outer_sum(self_score_grad, queries),
            outer_sum(self_probs.astype(low), grads),
        )
        refs = (
            query_grad_ref, key_grad_ref, value_grad_ref, self_key_grad_ref, self_value_grad_ref
        )
        for ref, term in zip(refs, terms):
            if image == 0:
                ref[...] = term
            else:
                ref[...] += term


def resample_back(queries, keys, values, self_keys, self_values, ids, grads, images):
    rows = keys.shape[0]
    shapes = [(LATENTS, LANES), (rows, LANES), (rows, LANES), (LATENTS, LANES), (LATENTS, LANES)]
    return pl.pallas_call(
        functools.partial(resample_back_kernel, images=images),
        out_shape=[jax.ShapeDtypeStruct(shape, wide) for shape in shapes],
        compiler_params=pltpu.CompilerParams(vmem_limit_bytes=vmem_bytes),
        name="resampler_attend_back",
    )(queries, keys, values, self_keys, self_values, ids, grads)


def lane_pad(array):
    gap = [(0, 0)] * (array.ndim - 1) + [(0, LANES - array.shape[-1])]
    return jnp.pad(array, gap)


def on_device(
    tokens, segment_ids, ln1_gain, ln1_bias, qkv_weight, q_bias, v_bias, out_weight, out_bias,
    ln2_gain, ln2_bias, fc1_weight, fc1_bias, fc2_weight, fc2_bias, bridge_gate, bridge_up,
    bridge_down, context_gain, latents, latent_gain, query_weight, key_weight, value_weight,
    mixer_weight, post_gain, latent_gate, latent_up, latent_down, cotangent,
):
    blocks = lax.axis_size("blk")
    planes = lax.axis_size("grp")
    me = lax.axis_index("blk")
    plane = lax.axis_index("grp")
    rows, features = tokens.shape
    pack_rows = rows * blocks
    hidden_units = fc1_weight.shape[1]
    unit_share = -(-hidden_units // blocks)
    model = latents.shape[1]
    model_share = query_weight.shape[0]
    lat_rows = cotangent.shape[0]
    lat_own = lat_rows // blocks
    images = lat_rows // LATENTS
    copies = blocks // HEADS
    head = me // copies
    part = me % copies
    kv_head = head // (P_HEADS // P_KV)

    def other_plane(array, step=1):
        return lax.ppermute(array, "grp", [(k, (k + step) % planes) for k in range(planes)])

    def both_planes(array):
        pieces = [array] + [other_plane(array, step) for step in range(1, planes)]
        return jnp.concatenate(
            [
                functools.reduce(
                    lambda held, step: jnp.where((plane - step) % planes == k, pieces[step], held),
                    range(1, planes),
                    pieces[0],
                )
                for k in range(planes)
            ],
            axis=0,
        )

    def plane_sum(array):
        mine = array.astype(low)
        total = mine.astype(wide)
        for step in range(1, planes):
            total = total + other_plane(mine, step).astype(wide)
        return total

    def to_columns(weight):
        padded = jnp.pad(weight, ((0, 0), (0, unit_share * blocks - weight.shape[1])))
        pieces = padded.reshape(weight.shape[0], blocks, unit_share)
        return swap_pieces(jnp.transpose(pieces, (1, 0, 2)))

    def share_rows(matrix):
        width = matrix.shape[0] // planes
        total = None
        for step in range(planes):
            piece = rows_at(matrix, (plane + step) % planes * width, width).astype(low)
            pairs = [
                (k * blocks + j, planes * j + (k + step) % planes)
                for k in range(planes)
                for j in range(blocks)
            ]
            arrived = lax.ppermute(piece, ("grp", "blk"), pairs).astype(wide)
            total = arrived if total is None else total + arrived
        return total

    def share_columns(matrix):
        width = matrix.shape[0] // planes
        total = rows_at(matrix, plane * width, width)
        for step in range(1, planes):
            piece = rows_at(matrix, (plane + step) % planes * width, width)
            total = total + other_plane(piece.astype(low), step).astype(wide)
        arrived = swap_pieces(total.astype(low).reshape(blocks, width // blocks, -1))
        return arrived.reshape(blocks, width // blocks, -1).astype(wide)

    head_pieces = lane_pad(qkv_weight.reshape(-1, 3, HEADS, HEAD))
    head_pieces = jnp.transpose(head_pieces, (2, 0, 1, 3)).reshape(HEADS, -1, 3 * LANES)
    head_weight = swap_pieces(jnp.repeat(head_pieces, copies, axis=0))
    fc1_own = to_columns(fc1_weight)
    fc2_own = to_columns(fc2_weight)
    mixer_pieces = jnp.transpose(
        mixer_weight.reshape(-1, blocks, model // blocks), (1, 0, 2)
    )
    mixer_own = swap_pieces(mixer_pieces)
    out_full = gather(out_weight)
    pair_weight = gather(jnp.concatenate([key_weight, value_weight], axis=1))
    fc1_bias_own = rows_at(
        jnp.pad(fc1_bias, (0, unit_share * blocks - hidden_units)), me * unit_share, unit_share
    )
    head_bias = jnp.concatenate(
        [
            lane_pad(rows_at(q_bias, head * HEAD, HEAD)),
            jnp.zeros((LANES,), wide),
            lane_pad(rows_at(v_bias, head * HEAD, HEAD)),
        ]
    )

    inputs = tokens.astype(wide)
    normed, first_norm_back = jax.vjp(layer_norm, inputs, ln1_gain, ln1_bias)
    first_rows = gather(normed.astype(low))
    all_ids = gather(segment_ids)
    row_ids = all_ids[:, None]
    col_ids = all_ids[None, :]
    heads = (mat_times(first_rows, head_weight) + head_bias).astype(low)
    attended_head = attend(heads, row_ids, col_ids)
    attended_pieces = swap_pieces(attended_head[:, :HEAD].reshape(blocks, rows, HEAD))
    attended_pieces = attended_pieces.reshape(blocks, rows, HEAD)[::copies]
    attended = jnp.transpose(attended_pieces, (1, 0, 2)).reshape(rows, features)
    hidden_state = inputs + mat_times(attended, out_full) + out_bias

    second, second_norm_back = jax.vjp(layer_norm, hidden_state, ln2_gain, ln2_bias)
    second_rows = gather(second.astype(low))
    pre = mat_times(second_rows, fc1_own) + fc1_bias_own
    act, gate_back = jax.vjp(smooth_gate, pre)
    act_low = act.astype(low)
    encoded = hidden_state + scatter_sum(mat_times_t(act_low, fc2_own)) + fc2_bias

    bridge_rows = gather(encoded.astype(low))
    bridge_act, bridge_act_back = jax.vjp(
        swiglu, mat_times(bridge_rows, bridge_gate), mat_times(bridge_rows, bridge_up)
    )
    bridge_hidden = bridge_act.astype(low)
    context = scatter_sum(mat_times(bridge_hidden, bridge_down))

    context_normed, context_norm_back = jax.vjp(rms_norm, context, context_gain)
    context_in = context_normed.astype(low)
    patch_pairs = gather(mat_times(context_in, pair_weight).astype(low))
    latent_normed, latent_norm_back = jax.vjp(rms_norm, latents.astype(wide), latent_gain)
    latent_in = latent_normed.astype(low)
    latent_in_own = rows_at(latent_in, me * model_share, model_share, 1)
    latent_proj = lax.psum(
        jnp.concatenate(
            [
                mat_times(latent_in_own, query_weight),
                mat_times(latent_in_own, key_weight),
                mat_times(latent_in_own, value_weight),
            ],
            axis=1,
        ),
        "blk",
    ).astype(low)
    query_width = P_HEADS * P_HEAD
    pair_width = P_KV * P_HEAD

    def head_of(matrix, first, index):
        return lane_pad(rows_at(matrix, first + index * P_HEAD, P_HEAD, 1))

    latent_query = head_of(latent_proj, 0, head)
    latent_key = head_of(latent_proj, query_width, kv_head)
    latent_value = head_of(latent_proj, query_width + pair_width, kv_head)
    patch_key = head_of(patch_pairs, 0, kv_head)
    patch_value = head_of(patch_pairs, pair_width, kv_head)
    attended_latent_head = resample(
        latent_query, patch_key, patch_value, latent_key, latent_value, col_ids, images
    )[:, :P_HEAD]
    attended_latent = gather(attended_latent_head).reshape(blocks, lat_rows, P_HEAD)[::copies]
    attended_latent = jnp.transpose(attended_latent, (1, 0, 2)).reshape(lat_rows, query_width)
    mixed = gather(mat_times(attended_latent, mixer_own).astype(low))
    mixed = jnp.transpose(mixed.reshape(blocks, lat_rows, -1), (1, 0, 2)).reshape(lat_rows, model)
    latent_state = jnp.tile(latents.astype(wide), (images, 1)) + mixed.astype(wide)

    post_in = rms_norm(latent_state, post_gain).astype(low)
    latent_act, latent_act_back = jax.vjp(
        swiglu, mat_times(post_in, latent_gate), mat_times(post_in, latent_up)
    )
    latent_hidden = latent_act.astype(low)
    own_start = me * lat_own
    state_own = rows_at(latent_state, own_start, lat_own)
    latent_gate_grad, latent_up_grad = latent_act_back(mat_times_t(cotangent, latent_down))
    latent_gate_low = latent_gate_grad.astype(low)
    latent_up_low = latent_up_grad.astype(low)
    post_grad = scatter_sum(
        mat_times_t(latent_gate_low, latent_gate) + mat_times_t(latent_up_low, latent_up)
    )
    _, post_norm_back = jax.vjp(rms_norm, state_own, post_gain)
    state_norm_grad, post_gain_part = post_norm_back(post_grad)
    state_grad = rows_at(cotangent, own_start, lat_own).astype(wide) + state_norm_grad
    state_low = gather(state_grad.astype(low))
    resid_part = lax.dynamic_update_slice_in_dim(
        jnp.zeros((LATENTS, model), wide), state_grad, own_start % LATENTS, 0
    )
    latents_out = (state_own + scatter_sum(mat_times(latent_hidden, latent_down))).astype(low)

    latent_att_grad = mat_times_t(state_low, mixer_weight).astype(low)
    if copies > 1:
        latent_att_grad = gather(latent_att_grad).reshape(blocks, lat_rows, -1)
        latent_att_grad = jnp.transpose(latent_att_grad, (1, 0, 2)).reshape(lat_rows, query_width)
        latent_att_grad = rows_at(latent_att_grad, head * P_HEAD, P_HEAD, 1)
    query_part, patch_key_part, patch_value_part, latent_key_part, latent_value_part = (
        resample_back(
            latent_query, patch_key, patch_value, latent_key, latent_value, col_ids,
            lane_pad(latent_att_grad), images,
        )
    )
    scale_latent = P_HEAD ** (-0.5)
    patch_part = jnp.concatenate(
        [patch_key_part[:, :P_HEAD] * scale_latent, patch_value_part[:, :P_HEAD]], axis=1
    ).astype(low)
    patch_part = swap_pieces(patch_part.reshape(blocks, rows, 2 * P_HEAD))
    patch_part = patch_part.reshape(blocks, rows, 2, P_HEAD)[::copies].astype(wide)
    patch_grad = jnp.sum(
        patch_part.reshape(P_KV, P_HEADS // P_KV, rows, 2, P_HEAD), axis=1
    )
    patch_grad = jnp.transpose(patch_grad, (1, 2, 0, 3)).reshape(rows, 2 * pair_width).astype(low)
    context_grad, context_gain_part = context_norm_back(mat_times_t(patch_grad, pair_weight))

    context_rows = gather(context_grad.astype(low))
    bridge_gate_grad, bridge_up_grad = bridge_act_back(mat_times_t(context_rows, bridge_down))
    bridge_gate_low = bridge_gate_grad.astype(low)
    bridge_up_low = bridge_up_grad.astype(low)
    grad_bridge_down = plane_sum(outer_sum(bridge_hidden, context_rows))
    encoded_grad = scatter_sum(
        mat_times_t(bridge_gate_low, bridge_gate) + mat_times_t(bridge_up_low, bridge_up)
    )
    grad_bridge_gate = plane_sum(outer_sum(bridge_rows, bridge_gate_low))
    grad_bridge_up = plane_sum(outer_sum(bridge_rows, bridge_up_low))

    encoded_rows = gather(encoded_grad.astype(low))
    grad_fc2_bias = jnp.sum(encoded_grad, axis=0)
    pre_grad = gate_back(mat_times(encoded_rows, fc2_own))[0].astype(low)
    second_grad = scatter_sum(mat_times_t(pre_grad, fc1_own))
    grad_fc1_bias = jnp.sum(pre_grad.astype(wide), axis=0)
    hidden_norm_grad, grad_ln2_gain, grad_ln2_bias = second_norm_back(second_grad)
    hidden_grad = encoded_grad + hidden_norm_grad
    grad_out_bias = jnp.sum(hidden_grad, axis=0)
    hidden_low = hidden_grad.astype(low)

    attended_grad = mat_times_t(hidden_low, out_full).astype(low)
    attended_grad = jnp.transpose(attended_grad.reshape(rows, HEADS, HEAD), (1, 0, 2))
    attended_grad = swap_pieces(jnp.repeat(lane_pad(attended_grad), copies, axis=0))
    query_low, key_low, value_low = attend_back(heads, attended_grad, row_ids, col_ids)
    head_grad = jnp.concatenate([query_low, key_low, value_low], axis=1)
    first_part = mat_times_t(head_grad, head_weight)
    if copies > 1:
        first_part = jnp.where(part == 0, first_part, 0.0)
    first_grad = scatter_sum(first_part)
    input_norm_grad, grad_ln1_gain, grad_ln1_bias = first_norm_back(first_grad)
    grad_tokens = hidden_grad + input_norm_grad

    hidden_rows = gather(hidden_low)
    out_width = out_weight.shape[0]
    grad_out = share_rows(
        outer_sum(rows_at(attended_head, part * out_width, out_width, 1), hidden_rows)
    )
    mixer_width = mixer_weight.shape[0]
    grad_mixer = share_rows(
        outer_sum(rows_at(attended_latent_head, part * mixer_width, mixer_width, 1), state_low)
    )
    grad_fc1 = outer_sum(second_rows, pre_grad)
    grad_fc2 = outer_sum(encoded_rows, act_low)
    units = share_columns(jnp.concatenate([grad_fc1, grad_fc2], axis=1))
    units = jnp.transpose(
        units.reshape(blocks, units.shape[1], 2, unit_share), (2, 1, 0, 3)
    ).reshape(2, units.shape[1], -1)[:, :, :hidden_units]
    grad_qkv = share_columns(outer_sum(first_rows, head_grad))[::copies]
    grad_qkv = grad_qkv.reshape(HEADS, grad_qkv.shape[1], 3, LANES)[..., :HEAD]
    grad_qkv = jnp.transpose(grad_qkv, (1, 2, 0, 3)).reshape(-1, 3 * features)
    context_in_columns = swap_pieces(
        jnp.transpose(context_in.reshape(rows, blocks, model_share), (1, 0, 2))
    )
    grad_pair = share_rows(outer_sum(context_in_columns, gather(patch_grad)))

    post_both = both_planes(post_in)
    grad_latent_gate = outer_sum(post_both, both_planes(latent_gate_low))
    grad_latent_up = outer_sum(post_both, both_planes(latent_up_low))
    grad_latent_down = outer_sum(both_planes(latent_hidden), both_planes(cotangent))

    once = (part == 0).astype(wide)

    def placed(width, pieces):
        base = jnp.zeros((LATENTS, width), wide)
        return lax.dynamic_update_slice_in_dim(base, pieces[0][:, :P_HEAD] * once, pieces[1], 1)

    def spread(width, piece, first):
        return lax.dynamic_update_slice_in_dim(jnp.zeros((width,), wide), piece, first, 0)

    latent_sums = lax.psum(
        (
            placed(query_width, (query_part, head * P_HEAD)),
            placed(pair_width, (latent_key_part, kv_head * P_HEAD)),
            placed(pair_width, (latent_value_part, kv_head * P_HEAD)),
            resid_part,
            context_gain_part,
            post_gain_part,
        ),
        ("grp", "blk"),
    )
    query_bias_part = jnp.sum(query_low[:, :HEAD].astype(wide), axis=0) * once
    value_bias_part = jnp.sum(value_low[:, :HEAD].astype(wide), axis=0) * once
    small = lax.psum(
        (
            grad_ln1_gain,
            grad_ln1_bias,
            spread(features, query_bias_part, head * HEAD),
            spread(features, value_bias_part, head * HEAD),
            grad_out_bias,
            grad_ln2_gain,
            grad_ln2_bias,
            spread(unit_share * blocks, grad_fc1_bias, me * unit_share),
            grad_fc2_bias,
        ),
        ("grp", "blk"),
    )

    query_grad = (latent_sums[0] * scale_latent).astype(low)
    pair_grad = jnp.concatenate([latent_sums[1] * scale_latent, latent_sums[2]], axis=1)
    pair_grad = pair_grad.astype(low)
    latent_in_grad = (
        mat_times_t(query_grad, query_weight)
        + mat_times_t(pair_grad[:, :pair_width], key_weight)
        + mat_times_t(pair_grad[:, pair_width:], value_weight)
    )
    latent_in_grad = gather(latent_in_grad).reshape(blocks, LATENTS, model_share)
    latent_in_grad = jnp.transpose(latent_in_grad, (1, 0, 2)).reshape(LATENTS, model)
    latent_grad, grad_latent_gain = latent_norm_back(latent_in_grad)
    grad_latents = latent_sums[3] + latent_grad
    share = model // (planes * blocks)
    latent_in_share = rows_at(latent_in, (plane * blocks + me) * share, share, 1)
    grad_query = outer_sum(latent_in_share, query_grad)
    grad_pair = grad_pair + outer_sum(latent_in_share, pair_grad)
    return (
        latents_out,
        grad_tokens,
        small[0],
        small[1],
        grad_qkv,
        small[2],
        small[3],
        grad_out,
        small[4],
        small[5],
        small[6],
        units[0],
        small[7][:hidden_units],
        units[1],
        small[8],
        grad_bridge_gate,
        grad_bridge_up,
        grad_bridge_down,
        latent_sums[4],
        grad_latents,
        grad_latent_gain,
        grad_query,
        grad_pair[:, :pair_width],
        grad_pair[:, pair_width:],
        grad_mixer,
        latent_sums[5],
        grad_latent_gate,
        grad_latent_up,
        grad_latent_down,
    )


def solution(mesh):
    in_specs = (
        P(("grp", "blk"), None),
        P(("grp", "blk")),
        P(),
        P(),
        P("blk", None),
        P(),
        P(),
        P("blk", None),
        P(),
        P(),
        P(),
        P("blk", None),
        P(),
        P("blk", None),
        P(),
        P(None, "blk"),
        P(None, "blk"),
        P("blk", None),
        P(),
        P(),
        P(),
        P("blk", None),
        P("blk", None),
        P("blk", None),
        P("blk", None),
        P(),
        P(None, "blk"),
        P(None, "blk"),
        P("blk", None),
        P("grp", None),
    )
    out_specs = (
        P(("grp", "blk"), None),
        P(("grp", "blk"), None),
        P(),
        P(),
        P(("grp", "blk"), None),
        P(),
        P(),
        P(("grp", "blk"), None),
        P(),
        P(),
        P(),
        P(("grp", "blk"), None),
        P(),
        P(("grp", "blk"), None),
        P(),
        P(None, "blk"),
        P(None, "blk"),
        P("blk", None),
        P(),
        P(),
        P(),
        P(("grp", "blk"), None),
        P(("grp", "blk"), None),
        P(("grp", "blk"), None),
        P(("grp", "blk"), None),
        P(),
        P(None, "blk"),
        P(None, "blk"),
        P("blk", None),
    )
    return jax.shard_map(
        on_device, mesh=mesh, in_specs=in_specs, out_specs=out_specs, check_vma=False
    )
```

```python
import functools

import jax
import jax.numpy as jnp
from jax import lax
from jax.experimental import pallas as pl
from jax.experimental.pallas import tpu as pltpu
from jax.sharding import PartitionSpec as P

HEADS = 16
HEAD = 72
LATENTS = 64
P_HEADS = 16
P_KV = 4
P_HEAD = 96
LANES = 128

masked_score = -1e30
norm_eps = 1e-06
vmem_bytes = 56 * 2**20
low = jnp.bfloat16
wide = jnp.float32


def layer_norm(values, gain, bias):
    center = values - jnp.mean(values, axis=-1, keepdims=True)
    spread = jnp.mean(center * center, axis=-1, keepdims=True)
    return center * lax.rsqrt(spread + norm_eps) * gain + bias


def rms_norm(values, gain):
    return values * lax.rsqrt(jnp.mean(values * values, axis=-1, keepdims=True) + norm_eps) * gain


def smooth_gate(values):
    return jax.nn.gelu(values, approximate=True)


def swiglu(gate, up):
    return jax.nn.silu(gate) * up


def mat_times(left, right):
    return jnp.dot(left, right, preferred_element_type=wide)


def contract(left, right, left_dim, right_dim):
    return lax.dot_general(
        left, right, (((left_dim,), (right_dim,)), ((), ())), preferred_element_type=wide
    )


def mat_times_t(left, right):
    return contract(left, right, 1, 1)


def outer_sum(left, right):
    return contract(left, right, 0, 0)


def rows_at(array, first, width, axis=0):
    return lax.dynamic_slice_in_dim(array, first, width, axis)


def gather(array):
    return lax.all_gather(array, "blk", axis=0, tiled=True)


def swiglu_back(gate, up, grad):
    share = jax.nn.sigmoid(gate)
    gated = gate * share
    return grad * up * (share + gated * (1.0 - share)), grad * gated


def scatter_sum(array):
    return lax.psum_scatter(array.astype(low), "blk", scatter_dimension=0, tiled=True).astype(wide)


def swap_pieces(pieces):
    flat = pieces.reshape((-1,) + pieces.shape[2:])
    return lax.all_to_all(flat, "blk", 0, 0, tiled=True)


def after(value, *others):
    return lax.optimization_barrier((value,) + others)[0]


def chip_walk(chips):
    return list(range(0, chips, 2)) + list(range(chips - 1, 0, -2))


class Walk:
    def __init__(self, blocks):
        self.blocks = blocks
        self.chips = blocks // 2
        self.short = blocks % 4 == 0 and self.chips <= 8
        self.far = self.chips // 2
        self.order = chip_walk(self.chips)
        me = lax.axis_index("blk")
        self.core = me % 2
        place = jnp.array([self.order.index(chip) for chip in range(self.chips)], jnp.int32)[me // 2]
        steps = jnp.arange(self.chips, dtype=jnp.int32) * (1 - 2 * self.core)
        self.ahead = jnp.array(self.order, jnp.int32)[(place + steps) % self.chips]
        places = [0]
        for step in range(1, self.far):
            places += [-step, step]
        self.places = places + [self.far]

    def advance(self, array):
        pairs = []
        for k in range(self.chips):
            pairs.append((2 * self.order[k], 2 * self.order[(k + 1) % self.chips]))
            pairs.append((2 * self.order[k] + 1, 2 * self.order[(k - 1) % self.chips] + 1))
        return lax.ppermute(array, "blk", pairs)

    def swap(self, array):
        return lax.ppermute(array, "blk", [(k, k ^ 1) for k in range(self.blocks)])

    def first_rows(self, index, rows):
        place = self.places[index]
        sibling_first = place > 0 and place != self.far
        cores = (1 - self.core, self.core) if sibling_first else (self.core, 1 - self.core)
        chip = self.ahead[place % self.chips]
        return [(2 * chip + core) * rows for core in cores]

    def spread(self, array):
        if not self.short:
            return [lax.all_gather(array, "blk", axis=0, tiled=True)]
        rows = array.shape[0]
        chain = jnp.concatenate([array, self.swap(array)], axis=0)
        found = [chain]
        for _ in range(1, self.far):
            chain = self.advance(chain)
            found += [chain, self.swap(chain)]
        end = self.advance(chain[:rows])
        return found + [jnp.concatenate([end, self.swap(end)], axis=0)]

    def gather(self, array):
        if not self.short:
            return lax.all_gather(array, "blk", axis=0, tiled=True)
        rows = array.shape[0]
        whole = jnp.zeros((self.blocks * rows,) + array.shape[1:], array.dtype)
        for index, block in enumerate(self.spread(array)):
            for half, first in enumerate(self.first_rows(index, rows)):
                piece = block[half * rows : (half + 1) * rows]
                whole = lax.dynamic_update_slice_in_dim(whole, piece, first, 0)
        return whole

    def collect(self, part, chunks=1):
        if not self.short:
            return scatter_sum(part(0))

        def total(kept, given):
            return kept.astype(wide) + self.swap(given.astype(low)).astype(wide)

        def split(block):
            width = block.shape[1] // chunks
            return [block[:, k * width : (k + 1) * width] for k in range(chunks)]

        block = part(2 * self.far - 1)
        rows = block.shape[0] // 2
        chains = [
            self.advance(total(piece[rows:], piece[:rows]).astype(low)) for piece in split(block)
        ]
        for step in range(self.far - 1, 0, -1):
            ahead, behind = split(part(2 * step)), split(part(2 * step - 1))
            for k in range(chunks):
                terms = total(ahead[k], behind[k])
                arrived = chains[k].astype(wide)
                if step == self.far - 1:
                    terms = jnp.concatenate([terms[:rows] + arrived, terms[rows:]], axis=0)
                else:
                    terms = terms + arrived
                chains[k] = self.advance(terms.astype(low))
        sums = [
            total(own[:rows] + chain[rows:].astype(wide), own[rows:] + chain[:rows].astype(wide))
            for own, chain in zip(split(part(0)), chains)
        ]
        return sums[0] if chunks == 1 else jnp.concatenate(sums, axis=1)

    def collect_rows(self, part, pack_rows):
        if not self.short:
            return scatter_sum(part(lambda array: array))
        rows = pack_rows // self.blocks

        def of_block(index):
            firsts = self.first_rows(index, rows)
            return part(
                lambda array: jnp.concatenate(
                    [rows_at(array, first, rows) for first in firsts], axis=0
                )
            )

        return self.collect(of_block)


def sum_over_all(array, axes):
    for axis in axes:
        size = lax.axis_size(axis)
        step = 1
        while step < size:
            array = array + lax.ppermute(array, axis, [(k, k ^ step) for k in range(size)])
            step *= 2
    return array


def attend_kernel(query_ref, key_ref, value_ref, row_ids_ref, col_ids_ref, out_ref):
    scores = mat_times_t(query_ref[...], key_ref[...]) * HEAD ** (-0.5)
    mask = row_ids_ref[...] == col_ids_ref[...]
    scores = jnp.where(mask, scores, masked_score)
    top = jnp.max(scores, axis=-1, keepdims=True)
    weights = jnp.exp(scores - top)
    total = jnp.sum(weights, axis=-1, keepdims=True)
    probs = (weights * (1.0 / total)).astype(low)
    out_ref[...] = mat_times(probs, value_ref[...]).astype(low)


def query_rows_for(rows):
    return 256 if rows <= 2048 else 64


def attend(heads, row_ids, col_ids):
    rows = heads.shape[0]
    width = query_rows_for(rows)
    return pl.pallas_call(
        attend_kernel,
        out_shape=jax.ShapeDtypeStruct((rows, LANES), low),
        grid=(rows // width,),
        in_specs=[
            pl.BlockSpec((width, LANES), lambda i: (i, 0)),
            pl.BlockSpec((rows, LANES), lambda i: (0, 1)),
            pl.BlockSpec((rows, LANES), lambda i: (0, 2)),
            pl.BlockSpec((width, 1), lambda i: (i, 0)),
            pl.BlockSpec((1, rows), lambda i: (0, 0)),
        ],
        out_specs=pl.BlockSpec((width, LANES), lambda i: (i, 0)),
        compiler_params=pltpu.CompilerParams(vmem_limit_bytes=vmem_bytes),
        name="vision_attend",
    )(heads, heads, heads, row_ids, col_ids)


def attend_back_kernel(
    query_ref, key_ref, value_ref, grad_ref, row_ids_ref, col_ids_ref,
    query_grad_ref, key_grad_ref, value_grad_ref, key_sum, value_sum,
):
    step = pl.program_id(0)

    @pl.when(step == 0)
    def _():
        key_sum[...] = jnp.zeros_like(key_sum)
        value_sum[...] = jnp.zeros_like(value_sum)

    queries = query_ref[...]
    grads = grad_ref[...]
    scores = mat_times_t(key_ref[...], queries) * HEAD ** (-0.5)
    mask = row_ids_ref[...] == col_ids_ref[...]
    scores = jnp.where(mask, scores, masked_score)
    top = jnp.max(scores, axis=0, keepdims=True)
    weights = jnp.exp(scores - top)
    total = jnp.sum(weights, axis=0, keepdims=True)
    probs = weights * (1.0 / total)
    dprob = mat_times_t(value_ref[...], grads)
    delta = jnp.sum(probs * dprob, axis=0, keepdims=True)
    score_grad = (probs * (dprob - delta)).astype(low)
    key_sum[...] += mat_times(score_grad, queries)
    value_sum[...] += mat_times(probs.astype(low), grads)
    query_grad_ref[...] = (outer_sum(score_grad, key_ref[...]) * HEAD ** (-0.5)).astype(low)

    @pl.when(step == pl.num_programs(0) - 1)
    def _():
        key_grad_ref[...] = (key_sum[...] * HEAD ** (-0.5)).astype(low)
        value_grad_ref[...] = value_sum[...].astype(low)


def attend_back(heads, grads, row_ids, col_ids):
    rows = heads.shape[0]
    width = query_rows_for(rows)
    return pl.pallas_call(
        attend_back_kernel,
        out_shape=[jax.ShapeDtypeStruct((rows, LANES), low)] * 3,
        grid=(rows // width,),
        in_specs=[
            pl.BlockSpec((width, LANES), lambda i: (i, 0)),
            pl.BlockSpec((rows, LANES), lambda i: (0, 1)),
            pl.BlockSpec((rows, LANES), lambda i: (0, 2)),
            pl.BlockSpec((width, LANES), lambda i: (i, 0)),
            pl.BlockSpec((rows, 1), lambda i: (0, 0)),
            pl.BlockSpec((1, width), lambda i: (0, i)) if width % LANES == 0
            else pl.BlockSpec((None, 1, width), lambda i: (i, 0, 0)),
        ],
        out_specs=[
            pl.BlockSpec((width, LANES), lambda i: (i, 0)),
            pl.BlockSpec((rows, LANES), lambda i: (0, 0)),
            pl.BlockSpec((rows, LANES), lambda i: (0, 0)),
        ],
        scratch_shapes=[pltpu.VMEM((rows, LANES), wide)] * 2,
        compiler_params=pltpu.CompilerParams(vmem_limit_bytes=vmem_bytes),
        name="vision_attend_back",
    )(
        heads, heads, heads, grads, row_ids,
        col_ids if width % LANES == 0 else col_ids.reshape(rows // width, 1, width),
    )


def image_probs(scores, self_scores, mask):
    scores = jnp.where(mask, scores, masked_score)
    top = jnp.maximum(
        jnp.max(scores, axis=-1, keepdims=True), jnp.max(self_scores, axis=-1, keepdims=True)
    )
    weights = jnp.where(mask, jnp.exp(scores - top), 0.0)
    self_weights = jnp.exp(self_scores - top)
    total = jnp.sum(weights, axis=-1, keepdims=True) + jnp.sum(
        self_weights, axis=-1, keepdims=True
    )
    scale = 1.0 / total
    return weights * scale, self_weights * scale


def resample_kernel(
    query_ref, key_ref, value_ref, self_key_ref, self_value_ref, ids_ref, out_ref, *, images
):
    queries = query_ref[...]
    scores = mat_times_t(queries, key_ref[...]) * P_HEAD ** (-0.5)
    self_scores = mat_times_t(queries, self_key_ref[...]) * P_HEAD ** (-0.5)
    for image in range(images):
        probs, self_probs = image_probs(scores, self_scores, ids_ref[...] == image)
        mixed = mat_times(probs.astype(low), value_ref[...])
        mixed += mat_times(self_probs.astype(low), self_value_ref[...])
        out_ref[pl.ds(image * LATENTS, LATENTS), :] = mixed.astype(low)


def resample(queries, keys, values, self_keys, self_values, ids, images):
    return pl.pallas_call(
        functools.partial(resample_kernel, images=images),
        out_shape=jax.ShapeDtypeStruct((images * LATENTS, LANES), low),
        compiler_params=pltpu.CompilerParams(vmem_limit_bytes=vmem_bytes),
        name="resampler_attend",
    )(queries, keys, values, self_keys, self_values, ids)


def resample_back_kernel(
    query_ref, key_ref, value_ref, self_key_ref, self_value_ref, ids_ref, grad_ref,
    query_grad_ref, key_grad_ref, value_grad_ref, self_key_grad_ref, self_value_grad_ref,
    *, images,
):
    queries = query_ref[...]
    scale = P_HEAD ** (-0.5)
    scores = mat_times_t(queries, key_ref[...]) * scale
    self_scores = mat_times_t(queries, self_key_ref[...]) * scale
    for image in range(images):
        probs, self_probs = image_probs(scores, self_scores, ids_ref[...] == image)
        grads = grad_ref[pl.ds(image * LATENTS, LATENTS), :]
        dprob = mat_times_t(grads, value_ref[...])
        self_dprob = mat_times_t(grads, self_value_ref[...])
        delta = jnp.sum(probs * dprob, axis=-1, keepdims=True) + jnp.sum(
            self_probs * self_dprob, axis=-1, keepdims=True
        )
        score_grad = (probs * (dprob - delta)).astype(low)
        self_score_grad = (self_probs * (self_dprob - delta)).astype(low)
        terms = (
            mat_times(score_grad, key_ref[...]) + mat_times(self_score_grad, self_key_ref[...]),
            outer_sum(score_grad, queries),
            outer_sum(probs.astype(low), grads),
            outer_sum(self_score_grad, queries),
            outer_sum(self_probs.astype(low), grads),
        )
        refs = (
            query_grad_ref, key_grad_ref, value_grad_ref, self_key_grad_ref, self_value_grad_ref
        )
        for ref, term in zip(refs, terms):
            if image == 0:
                ref[...] = term
            else:
                ref[...] += term


def resample_back(queries, keys, values, self_keys, self_values, ids, grads, images):
    rows = keys.shape[0]
    shapes = [(LATENTS, LANES), (rows, LANES), (rows, LANES), (LATENTS, LANES), (LATENTS, LANES)]
    return pl.pallas_call(
        functools.partial(resample_back_kernel, images=images),
        out_shape=[jax.ShapeDtypeStruct(shape, wide) for shape in shapes],
        compiler_params=pltpu.CompilerParams(vmem_limit_bytes=vmem_bytes),
        name="resampler_attend_back",
    )(queries, keys, values, self_keys, self_values, ids, grads)


def lane_pad(array):
    gap = [(0, 0)] * (array.ndim - 1) + [(0, LANES - array.shape[-1])]
    return jnp.pad(array, gap)


def on_device(
    tokens, segment_ids, ln1_gain, ln1_bias, qkv_weight, q_bias, v_bias, out_weight, out_bias,
    ln2_gain, ln2_bias, fc1_weight, fc1_bias, fc2_weight, fc2_bias, bridge_gate, bridge_up,
    bridge_down, context_gain, latents, latent_gain, query_weight, key_weight, value_weight,
    mixer_weight, post_gain, latent_gate, latent_up, latent_down, cotangent,
):
    blocks = lax.axis_size("blk")
    planes = lax.axis_size("grp")
    me = lax.axis_index("blk")
    plane = lax.axis_index("grp")
    rows, features = tokens.shape
    pack_rows = rows * blocks
    hidden_units = fc1_weight.shape[1]
    unit_share = -(-hidden_units // blocks)
    model = latents.shape[1]
    model_share = query_weight.shape[0]
    lat_rows = cotangent.shape[0]
    lat_own = lat_rows // blocks
    images = lat_rows // LATENTS
    copies = blocks // HEADS
    head = me // copies
    part = me % copies
    kv_head = head // (P_HEADS // P_KV)
    walk = Walk(blocks)

    def other_plane(array, step=1):
        return lax.ppermute(array, "grp", [(k, (k + step) % planes) for k in range(planes)])

    def both_planes(array):
        pieces = [array] + [other_plane(array, step) for step in range(1, planes)]
        return jnp.concatenate(
            [
                functools.reduce(
                    lambda held, step: jnp.where((plane - step) % planes == k, pieces[step], held),
                    range(1, planes),
                    pieces[0],
                )
                for k in range(planes)
            ],
            axis=0,
        )

    def joined(blocks):
        return blocks[0] if len(blocks) == 1 else jnp.concatenate(blocks, axis=0)

    def to_columns(weight):
        padded = jnp.pad(weight, ((0, 0), (0, unit_share * blocks - weight.shape[1])))
        return jnp.transpose(padded.reshape(weight.shape[0], blocks, unit_share), (1, 0, 2))

    def share_rows(matrix):
        width = matrix.shape[0] // planes
        total = None
        for step in range(planes):
            piece = rows_at(matrix, (plane + step) % planes * width, width).astype(low)
            pairs = [
                (k * blocks + j, planes * j + (k + step) % planes)
                for k in range(planes)
                for j in range(blocks)
            ]
            arrived = lax.ppermute(piece, ("grp", "blk"), pairs).astype(wide)
            total = arrived if total is None else total + arrived
        return total

    def share_columns(matrix, last):
        width = matrix.shape[0] // (planes * blocks)
        pieces = matrix.astype(low).reshape(planes, blocks, width, -1)
        arrived = swap_pieces(jnp.transpose(pieces, (1, 0, 2, 3)))
        arrived = arrived.reshape(blocks, planes, width, -1)
        arrived = after(arrived, last)
        total = lax.dynamic_index_in_dim(arrived, plane, 1, keepdims=False).astype(wide)
        for step in range(1, planes):
            piece = lax.dynamic_index_in_dim(
                arrived, (plane + step) % planes, 1, keepdims=False
            )
            total = total + other_plane(piece, step).astype(wide)
        return total

    head_pieces = lane_pad(qkv_weight.reshape(-1, 3, HEADS, HEAD))
    head_pieces = jnp.transpose(head_pieces, (2, 0, 1, 3)).reshape(HEADS, -1, 3 * LANES)
    head_weight = swap_pieces(jnp.repeat(head_pieces, copies, axis=0))
    fc1_bias_own = rows_at(
        jnp.pad(fc1_bias, (0, unit_share * blocks - hidden_units)), me * unit_share, unit_share
    )
    head_bias = jnp.concatenate(
        [
            lane_pad(rows_at(q_bias, head * HEAD, HEAD)),
            jnp.zeros((LANES,), wide),
            lane_pad(rows_at(v_bias, head * HEAD, HEAD)),
        ]
    )

    inputs = tokens.astype(wide)
    normed, first_norm_back = jax.vjp(layer_norm, inputs, ln1_gain, ln1_bias)
    first_rows = walk.gather(normed.astype(low))
    all_ids = swap_pieces(jnp.tile(segment_ids[None, None], (blocks, 1, 1))).reshape(-1)
    cotangent_both = both_planes(after(cotangent, first_rows))
    out_full = gather(after(out_weight, first_rows))
    pair_weight = gather(
        after(jnp.concatenate([key_weight, value_weight], axis=1), first_rows)
    )
    row_ids = all_ids[:, None]
    col_ids = all_ids[None, :]
    heads = (mat_times(first_rows, head_weight) + head_bias).astype(low)
    fc1_weight, fc2_weight = lax.optimization_barrier((fc1_weight, fc2_weight, first_rows))[:2]
    unit_weights = swap_pieces(
        jnp.concatenate([to_columns(fc1_weight), to_columns(fc2_weight)], axis=2)
    )
    fc1_own = unit_weights[:, :unit_share]
    fc2_own = unit_weights[:, unit_share:]
    attended_head = attend(heads, row_ids, col_ids)
    attended_pieces = swap_pieces(attended_head[:, :HEAD].reshape(blocks, rows, HEAD))
    attended_pieces = attended_pieces.reshape(blocks, rows, HEAD)[::copies]
    attended = jnp.transpose(attended_pieces, (1, 0, 2)).reshape(rows, features)
    hidden_state = inputs + mat_times(attended, out_full) + out_bias

    second, second_norm_back = jax.vjp(layer_norm, hidden_state, ln2_gain, ln2_bias)
    second_blocks = walk.spread(second.astype(low))
    pre_blocks = [mat_times(block, fc1_own) + fc1_bias_own for block in second_blocks]
    act_blocks = [smooth_gate(pre).astype(low) for pre in pre_blocks]
    encoded = walk.collect(lambda i: mat_times_t(act_blocks[i], fc2_own))
    encoded = after(hidden_state + encoded + fc2_bias, pair_weight, cotangent_both)

    bridge_blocks = walk.spread(encoded.astype(low))
    gate_blocks = [mat_times(block, bridge_gate) for block in bridge_blocks]
    up_blocks = [mat_times(block, bridge_up) for block in bridge_blocks]
    hidden_blocks = [swiglu(gate, up).astype(low) for gate, up in zip(gate_blocks, up_blocks)]
    context = walk.collect(lambda i: mat_times(hidden_blocks[i], bridge_down), 2)

    context_normed, context_norm_back = jax.vjp(rms_norm, context, context_gain)
    context_in = context_normed.astype(low)
    patch_pairs = walk.gather(mat_times(context_in, pair_weight).astype(low))
    latent_normed, latent_norm_back = jax.vjp(rms_norm, latents.astype(wide), latent_gain)
    latent_in = latent_normed.astype(low)
    latent_in_own = rows_at(latent_in, me * model_share, model_share, 1)
    query_width = P_HEADS * P_HEAD
    pair_width = P_KV * P_HEAD


    def heads_of(matrix, count):
        split = lane_pad(matrix.reshape(LATENTS, count, P_HEAD))
        split = jnp.transpose(split, (1, 0, 2))
        return jnp.repeat(split, blocks // count, axis=0)

    latent_pieces = jnp.concatenate(
        [
            heads_of(mat_times(latent_in_own, query_weight), P_HEADS),
            heads_of(mat_times(latent_in_own, key_weight), P_KV),
            heads_of(mat_times(latent_in_own, value_weight), P_KV),
        ],
        axis=2,
    ).astype(low)
    mixer_pieces = jnp.transpose(mixer_weight.reshape(-1, blocks, model // blocks), (1, 0, 2))
    latent_pieces, mixer_pieces = lax.optimization_barrier(
        (latent_pieces, mixer_pieces, second_blocks[-1])
    )[:2]
    latent_proj = swap_pieces(latent_pieces).reshape(blocks, LATENTS, 3 * LANES)
    latent_proj = jnp.sum(latent_proj.astype(wide), axis=0).astype(low)
    mixer_own = swap_pieces(mixer_pieces)
    latent_query = latent_proj[:, :LANES]
    latent_key = latent_proj[:, LANES : 2 * LANES]
    latent_value = latent_proj[:, 2 * LANES :]

    def head_of(matrix, first, index):
        return lane_pad(rows_at(matrix, first + index * P_HEAD, P_HEAD, 1))

    patch_key = head_of(patch_pairs, 0, kv_head)
    patch_value = head_of(patch_pairs, pair_width, kv_head)
    attended_latent_head = resample(
        latent_query, patch_key, patch_value, latent_key, latent_value, col_ids, images
    )[:, :P_HEAD]
    attended_latent = walk.gather(attended_latent_head).reshape(blocks, lat_rows, P_HEAD)[::copies]
    attended_latent = jnp.transpose(attended_latent, (1, 0, 2)).reshape(lat_rows, query_width)
    mixed = walk.gather(mat_times(attended_latent, mixer_own).astype(low))
    mixed = jnp.transpose(mixed.reshape(blocks, lat_rows, -1), (1, 0, 2)).reshape(lat_rows, model)
    latent_state = jnp.tile(latents.astype(wide), (images, 1)) + mixed.astype(wide)

    post_in = rms_norm(latent_state, post_gain).astype(low)
    latent_gate_pre = mat_times(post_in, latent_gate)
    latent_up_pre = mat_times(post_in, latent_up)
    latent_hidden = swiglu(latent_gate_pre, latent_up_pre).astype(low)
    own_start = me * lat_own
    state_own = rows_at(latent_state, own_start, lat_own)
    latent_gate_grad, latent_up_grad = swiglu_back(
        latent_gate_pre, latent_up_pre, mat_times_t(cotangent, latent_down)
    )
    latent_gate_low = latent_gate_grad.astype(low)
    latent_up_low = latent_up_grad.astype(low)
    post_part = mat_times_t(latent_gate_low, latent_gate) + mat_times_t(latent_up_low, latent_up)
    post_part = post_part.astype(low)
    post_grad = walk.collect_rows(lambda take: take(post_part), lat_rows)
    _, post_norm_back = jax.vjp(rms_norm, state_own, post_gain)
    state_norm_grad, post_gain_part = post_norm_back(post_grad)
    state_grad = rows_at(cotangent, own_start, lat_own).astype(wide) + state_norm_grad
    state_low = walk.gather(state_grad.astype(low))
    resid = jnp.sum(state_low.astype(wide).reshape(images, LATENTS, model), axis=0)
    resid_low = resid.astype(low)
    resid_others = [other_plane(resid_low, step) for step in range(1, planes)]
    latent_down_rows = scatter_sum(mat_times(latent_hidden, latent_down))

    latent_att_grad = mat_times_t(state_low, mixer_weight).astype(low)
    if copies > 1:
        latent_att_grad = gather(latent_att_grad).reshape(blocks, lat_rows, -1)
        latent_att_grad = jnp.transpose(latent_att_grad, (1, 0, 2)).reshape(lat_rows, query_width)
        latent_att_grad = rows_at(latent_att_grad, head * P_HEAD, P_HEAD, 1)
    query_part, patch_key_part, patch_value_part, latent_key_part, latent_value_part = (
        resample_back(
            latent_query, patch_key, patch_value, latent_key, latent_value, col_ids,
            lane_pad(latent_att_grad), images,
        )
    )
    scale_latent = P_HEAD ** (-0.5)
    patch_part = jnp.concatenate(
        [patch_key_part[:, :P_HEAD] * scale_latent, patch_value_part[:, :P_HEAD]], axis=1
    ).astype(low)
    patch_part = swap_pieces(patch_part.reshape(blocks, rows, 2 * P_HEAD))
    patch_part = patch_part.reshape(blocks, rows, 2, P_HEAD)[::copies].astype(wide)
    patch_grad = jnp.sum(
        patch_part.reshape(P_KV, P_HEADS // P_KV, rows, 2, P_HEAD), axis=1
    )
    patch_grad = jnp.transpose(patch_grad, (1, 2, 0, 3)).reshape(rows, 2 * pair_width).astype(low)
    context_grad, context_gain_part = context_norm_back(mat_times_t(patch_grad, pair_weight))

    units_both = both_planes(
        jnp.concatenate([latent_gate_low, latent_up_low, latent_hidden], axis=1)
    )
    post_both = both_planes(post_in)
    lat_units = latent_hidden.shape[1]
    mixer_width = mixer_weight.shape[0]
    grad_mixer = share_rows(
        outer_sum(rows_at(attended_latent_head, part * mixer_width, mixer_width, 1), state_low)
    )

    context_blocks = walk.spread(context_grad.astype(low))
    units_both = after(units_both, context_blocks[len(context_blocks) // 2])
    grad_latent_gate = outer_sum(post_both, units_both[:, :lat_units])
    grad_latent_up = outer_sum(post_both, units_both[:, lat_units : 2 * lat_units])
    grad_latent_down = outer_sum(units_both[:, 2 * lat_units :], cotangent_both)
    context_in_columns = swap_pieces(
        jnp.transpose(context_in.reshape(rows, blocks, model_share), (1, 0, 2))
    )
    patch_grad_rows = gather(patch_grad)
    grad_pair = share_rows(outer_sum(context_in_columns, patch_grad_rows))
    latent_table = jnp.concatenate(
        [query_part * scale_latent, latent_key_part * scale_latent, latent_value_part], axis=1
    )
    latent_total = latent_table
    for step in range(1, planes):
        latent_total = latent_total + other_plane(latent_table, step)
    part_bridge_down = outer_sum(joined(hidden_blocks), joined(context_blocks)).astype(low)
    part_bridge_down = after(part_bridge_down, grad_pair, grad_mixer, latent_total, resid_others)
    down_others = [other_plane(part_bridge_down, step) for step in range(1, planes)]
    context_blocks[-1] = after(context_blocks[-1], part_bridge_down)
    bridge_grads = [
        swiglu_back(gate, up, mat_times_t(block, bridge_down))
        for gate, up, block in zip(gate_blocks, up_blocks, context_blocks)
    ]
    gate_low_blocks = [gate.astype(low) for gate, _ in bridge_grads]
    up_low_blocks = [up.astype(low) for _, up in bridge_grads]
    encoded_grad = walk.collect(
        lambda i: mat_times_t(gate_low_blocks[i], bridge_gate)
        + mat_times_t(up_low_blocks[i], bridge_up)
    )
    bridge_rows = joined(bridge_blocks)
    part_bridge_gate = outer_sum(bridge_rows, joined(gate_low_blocks)).astype(low)
    part_bridge_up = outer_sum(bridge_rows, joined(up_low_blocks)).astype(low)
    part_bridge_pair = jnp.concatenate([part_bridge_gate, part_bridge_up], axis=1)
    pair_others = [other_plane(part_bridge_pair, step) for step in range(1, planes)]

    encoded_blocks = walk.spread(encoded_grad.astype(low))
    grad_fc2_bias = jnp.sum(encoded_grad, axis=0)
    pre_grad_blocks = [
        jax.vjp(smooth_gate, pre)[1](mat_times(block, fc2_own))[0].astype(low)
        for pre, block in zip(pre_blocks, encoded_blocks)
    ]
    second_grad = walk.collect(lambda i: mat_times_t(pre_grad_blocks[i], fc1_own))
    pre_grad = joined(pre_grad_blocks)
    grad_fc1_bias = jnp.sum(pre_grad.astype(wide), axis=0)
    hidden_norm_grad, grad_ln2_gain, grad_ln2_bias = second_norm_back(second_grad)
    hidden_grad = encoded_grad + hidden_norm_grad
    grad_out_bias = jnp.sum(hidden_grad, axis=0)
    hidden_low = hidden_grad.astype(low)

    attended_grad = mat_times_t(hidden_low, out_full).astype(low)
    attended_grad = jnp.transpose(attended_grad.reshape(rows, HEADS, HEAD), (1, 0, 2))
    attended_grad = swap_pieces(jnp.repeat(lane_pad(attended_grad), copies, axis=0))
    query_low, key_low, value_low = attend_back(heads, attended_grad, row_ids, col_ids)
    head_grad = jnp.concatenate([query_low, key_low, value_low], axis=1)
    first_weight = head_weight
    if copies > 1:
        first_weight = jnp.where(part == 0, head_weight, jnp.zeros((), low))
    first_grad = walk.collect_rows(
        lambda take: mat_times_t(take(head_grad), first_weight), pack_rows
    )
    input_norm_grad, grad_ln1_gain, grad_ln1_bias = first_norm_back(first_grad)
    grad_tokens = hidden_grad + input_norm_grad

    hidden_rows = gather(hidden_low)
    out_width = out_weight.shape[0]
    grad_out = outer_sum(rows_at(attended_head, part * out_width, out_width, 1), hidden_rows)
    grad_out = share_rows(after(grad_out, first_grad))
    grad_fc1 = outer_sum(joined(second_blocks), pre_grad)
    grad_fc2 = outer_sum(joined(encoded_blocks), joined(act_blocks))
    units = share_columns(jnp.concatenate([grad_fc1, grad_fc2], axis=1), first_grad)
    units = jnp.transpose(
        units.reshape(blocks, units.shape[1], 2, unit_share), (2, 1, 0, 3)
    ).reshape(2, units.shape[1], -1)[:, :, :hidden_units]
    grad_qkv = share_columns(outer_sum(first_rows, head_grad), first_grad)[::copies]
    grad_qkv = grad_qkv.reshape(HEADS, grad_qkv.shape[1], 3, LANES)[..., :HEAD]
    grad_qkv = jnp.transpose(grad_qkv, (1, 2, 0, 3)).reshape(-1, 3 * features)
    once = (part == 0).astype(wide)

    def spread(width, piece, first):
        return lax.dynamic_update_slice_in_dim(jnp.zeros((width,), wide), piece, first, 0)

    def packed(arrays):
        flat = jnp.concatenate([array.reshape(-1) for array in arrays])
        gap = -flat.shape[0] % (8 * LANES)
        return jnp.pad(flat, (0, gap)).reshape(-1, LANES)

    def unpacked(table, arrays):
        flat = table.reshape(-1)
        first = 0
        pieces = []
        for array in arrays:
            pieces.append(flat[first : first + array.size].reshape(array.shape))
            first += array.size
        return pieces

    query_bias_part = jnp.sum(query_low[:, :HEAD].astype(wide), axis=0) * once
    value_bias_part = jnp.sum(value_low[:, :HEAD].astype(wide), axis=0) * once
    small_terms = (
        grad_ln1_gain,
        grad_ln1_bias,
        spread(features, query_bias_part, head * HEAD),
        spread(features, value_bias_part, head * HEAD),
        grad_out_bias,
        grad_ln2_gain,
        grad_ln2_bias,
        spread(unit_share * blocks, grad_fc1_bias, me * unit_share),
        grad_fc2_bias,
        context_gain_part,
        post_gain_part,
    )
    small = unpacked(sum_over_all(packed(small_terms), ("grp", "blk")), small_terms)
    def plane_sum(mine, others):
        others = lax.optimization_barrier((others, first_grad))[0]
        return functools.reduce(
            lambda total, other: total + other.astype(wide), others, mine.astype(wide)
        )

    bridge_units = bridge_gate.shape[1]
    grad_bridge_down = plane_sum(part_bridge_down, down_others)
    grad_bridge_gate = plane_sum(
        part_bridge_gate, [other[:, :bridge_units] for other in pair_others]
    )
    grad_bridge_up = plane_sum(part_bridge_up, [other[:, bridge_units:] for other in pair_others])
    latents_out = (state_own + after(latent_down_rows, first_grad)).astype(low)

    latent_tables = walk.gather(after(latent_total, encoded_grad).astype(low))
    latent_tables = latent_tables.reshape(blocks, LATENTS, 3, LANES)[::copies, :, :, :P_HEAD]
    query_grad = jnp.transpose(latent_tables[:, :, 0], (1, 0, 2)).reshape(LATENTS, query_width)
    pair_grad = jnp.sum(
        latent_tables[:, :, 1:]
        .astype(wide)
        .reshape(P_KV, P_HEADS // P_KV, LATENTS, 2, P_HEAD),
        axis=1,
    )
    pair_grad = jnp.transpose(pair_grad, (1, 2, 0, 3)).reshape(LATENTS, 2 * pair_width)
    pair_grad = pair_grad.astype(low)
    latent_in_grad = (
        mat_times_t(query_grad, query_weight)
        + mat_times_t(pair_grad[:, :pair_width], key_weight)
        + mat_times_t(pair_grad[:, pair_width:], value_weight)
    )
    latent_in_grad = walk.gather(latent_in_grad).reshape(blocks, LATENTS, model_share)
    latent_in_grad = jnp.transpose(latent_in_grad, (1, 0, 2)).reshape(LATENTS, model)
    latent_grad, grad_latent_gain = latent_norm_back(latent_in_grad)
    grad_latents = latent_grad + plane_sum(resid_low, resid_others)
    share = model // (planes * blocks)
    latent_in_share = rows_at(latent_in, (plane * blocks + me) * share, share, 1)
    grad_query = outer_sum(latent_in_share, query_grad)
    grad_pair = grad_pair + outer_sum(latent_in_share, pair_grad)
    return (
        latents_out,
        grad_tokens,
        small[0],
        small[1],
        grad_qkv,
        small[2],
        small[3],
        grad_out,
        small[4],
        small[5],
        small[6],
        units[0],
        small[7][:hidden_units],
        units[1],
        small[8],
        grad_bridge_gate,
        grad_bridge_up,
        grad_bridge_down,
        small[9],
        grad_latents,
        grad_latent_gain,
        grad_query,
        grad_pair[:, :pair_width],
        grad_pair[:, pair_width:],
        grad_mixer,
        small[10],
        grad_latent_gate,
        grad_latent_up,
        grad_latent_down,
    )


def solution(mesh):
    in_specs = (
        P(("grp", "blk"), None),
        P(("grp", "blk")),
        P(),
        P(),
        P("blk", None),
        P(),
        P(),
        P("blk", None),
        P(),
        P(),
        P(),
        P("blk", None),
        P(),
        P("blk", None),
        P(),
        P(None, "blk"),
        P(None, "blk"),
        P("blk", None),
        P(),
        P(),
        P(),
        P("blk", None),
        P("blk", None),
        P("blk", None),
        P("blk", None),
        P(),
        P(None, "blk"),
        P(None, "blk"),
        P("blk", None),
        P("grp", None),
    )
    out_specs = (
        P(("grp", "blk"), None),
        P(("grp", "blk"), None),
        P(),
        P(),
        P(("grp", "blk"), None),
        P(),
        P(),
        P(("grp", "blk"), None),
        P(),
        P(),
        P(),
        P(("grp", "blk"), None),
        P(),
        P(("grp", "blk"), None),
        P(),
        P(None, "blk"),
        P(None, "blk"),
        P("blk", None),
        P(),
        P(),
        P(),
        P(("grp", "blk"), None),
        P(("grp", "blk"), None),
        P(("grp", "blk"), None),
        P(("grp", "blk"), None),
        P(),
        P(None, "blk"),
        P(None, "blk"),
        P("blk", None),
    )
    return jax.shard_map(
        on_device, mesh=mesh, in_specs=in_specs, out_specs=out_specs, check_vma=False
    )
```

```python
import functools

import jax
import jax.numpy as jnp
from jax import lax
from jax.experimental import pallas as pl
from jax.experimental.pallas import tpu as pltpu
from jax.sharding import PartitionSpec as P

HEADS = 16
HEAD = 72
LATENTS = 64
P_HEADS = 16
P_KV = 4
P_HEAD = 96
LANES = 128

masked_score = -1e30
norm_eps = 1e-06
vmem_bytes = 56 * 2**20
low = jnp.bfloat16
wide = jnp.float32


def layer_norm(values, gain, bias):
    center = values - jnp.mean(values, axis=-1, keepdims=True)
    spread = jnp.mean(center * center, axis=-1, keepdims=True)
    return center * lax.rsqrt(spread + norm_eps) * gain + bias


def rms_norm(values, gain):
    return values * lax.rsqrt(jnp.mean(values * values, axis=-1, keepdims=True) + norm_eps) * gain


def smooth_gate(values):
    return jax.nn.gelu(values, approximate=True)


def swiglu(gate, up):
    return jax.nn.silu(gate) * up


def mat_times(left, right):
    return jnp.dot(left, right, preferred_element_type=wide)


def contract(left, right, left_dim, right_dim):
    return lax.dot_general(
        left, right, (((left_dim,), (right_dim,)), ((), ())), preferred_element_type=wide
    )


def mat_times_t(left, right):
    return contract(left, right, 1, 1)


def outer_sum(left, right):
    return contract(left, right, 0, 0)


def rows_at(array, first, width, axis=0):
    return lax.dynamic_slice_in_dim(array, first, width, axis)


def gather(array):
    return lax.all_gather(array, "blk", axis=0, tiled=True)


def swiglu_back(gate, up, grad):
    share = jax.nn.sigmoid(gate)
    gated = gate * share
    return grad * up * (share + gated * (1.0 - share)), grad * gated


def scatter_sum(array):
    return lax.psum_scatter(array.astype(low), "blk", scatter_dimension=0, tiled=True).astype(wide)


def swap_pieces(pieces):
    flat = pieces.reshape((-1,) + pieces.shape[2:])
    return lax.all_to_all(flat, "blk", 0, 0, tiled=True)


def after(value, *others):
    return lax.optimization_barrier((value,) + others)[0]


def chip_walk(chips):
    return list(range(0, chips, 2)) + list(range(chips - 1, 0, -2))


class Walk:
    def __init__(self, blocks):
        self.blocks = blocks
        self.chips = blocks // 2
        self.short = blocks % 4 == 0 and self.chips <= 8
        self.far = self.chips // 2
        self.order = chip_walk(self.chips)
        me = lax.axis_index("blk")
        self.core = me % 2
        place = jnp.array([self.order.index(chip) for chip in range(self.chips)], jnp.int32)[me // 2]
        steps = jnp.arange(self.chips, dtype=jnp.int32) * (1 - 2 * self.core)
        self.ahead = jnp.array(self.order, jnp.int32)[(place + steps) % self.chips]
        places = [0]
        for step in range(1, self.far):
            places += [-step, step]
        self.places = places + [self.far]

    def advance(self, array):
        pairs = []
        for k in range(self.chips):
            pairs.append((2 * self.order[k], 2 * self.order[(k + 1) % self.chips]))
            pairs.append((2 * self.order[k] + 1, 2 * self.order[(k - 1) % self.chips] + 1))
        return lax.ppermute(array, "blk", pairs)

    def swap(self, array):
        return lax.ppermute(array, "blk", [(k, k ^ 1) for k in range(self.blocks)])

    def first_rows(self, index, rows):
        place = self.places[index]
        sibling_first = place > 0 and place != self.far
        cores = (1 - self.core, self.core) if sibling_first else (self.core, 1 - self.core)
        chip = self.ahead[place % self.chips]
        return [(2 * chip + core) * rows for core in cores]

    def spread(self, array, fill=()):
        if not self.short:
            for work in fill:
                work(array)
            return [lax.all_gather(array, "blk", axis=0, tiled=True)]
        rows = array.shape[0]
        chain = jnp.concatenate([array, self.swap(array)], axis=0)
        found = [chain]
        made = ()
        for step in range(1, self.far):
            sent = after(chain, *made) if made else chain
            chain = self.advance(sent)
            made = fill[step - 1](sent) if step <= len(fill) else ()
            found += [chain, self.swap(chain)]
        end = self.advance((after(chain, *made) if made else chain)[:rows])
        return found + [jnp.concatenate([end, self.swap(end)], axis=0)]

    def in_order(self, found):
        if not self.short:
            return found[0]
        rows = found[0].shape[0] // 2
        whole = jnp.zeros((self.blocks * rows,) + found[0].shape[1:], found[0].dtype)
        for index, block in enumerate(found):
            for half, first in enumerate(self.first_rows(index, rows)):
                piece = block[half * rows : (half + 1) * rows]
                whole = lax.dynamic_update_slice_in_dim(whole, piece, first, 0)
        return whole

    def gather(self, array, fill=()):
        return self.in_order(self.spread(array, fill))

    def in_own_order(self, array):
        if not self.short:
            return array
        rows = array.shape[0] // self.blocks
        firsts = [first for index in range(2 * self.far) for first in self.first_rows(index, rows)]
        return jnp.concatenate([rows_at(array, first, rows) for first in firsts], axis=0)

    def device_order(self):
        if not self.short:
            return jnp.arange(self.blocks, dtype=jnp.int32)
        return jnp.stack(
            [first for index in range(2 * self.far) for first in self.first_rows(index, 1)]
        )

    def collect(self, part, chunks=1, fill=()):
        if not self.short:
            terms = part(0)
            for work in fill:
                work(terms)
            return scatter_sum(terms)

        def total(kept, given, sent=()):
            given = given.astype(low)
            given = self.swap(after(given, *sent) if sent else given)
            return kept.astype(wide) + given.astype(wide)

        def split(block):
            width = block.shape[1] // chunks
            return [block[:, k * width : (k + 1) * width] for k in range(chunks)]

        block = part(2 * self.far - 1)
        rows = block.shape[0] // 2
        sent = tuple(total(piece[rows:], piece[:rows]).astype(low) for piece in split(block))
        chains = [self.advance(one) for one in sent]
        made = fill[0](sent[0]) if fill else ()
        for step in range(self.far - 1, 0, -1):
            ahead, behind = split(part(2 * step)), split(part(2 * step - 1))
            before, sent = sent, ()
            for k in range(chunks):
                terms = total(ahead[k], behind[k], before)
                arrived = chains[k].astype(wide)
                if step == self.far - 1:
                    terms = jnp.concatenate([terms[:rows] + arrived, terms[rows:]], axis=0)
                else:
                    terms = terms + arrived
                terms = terms.astype(low)
                sent += (after(terms, *made) if made else terms,)
                chains[k] = self.advance(sent[-1])
            made = fill[self.far - step](sent[0]) if self.far - step < len(fill) else ()
        sums = [
            total(own[:rows] + chain[rows:].astype(wide), own[rows:] + chain[:rows].astype(wide))
            for own, chain in zip(split(part(0)), chains)
        ]
        return sums[0] if chunks == 1 else jnp.concatenate(sums, axis=1)

    def collect_rows(self, part, pack_rows, fill=()):
        if not self.short:
            return self.collect(lambda _: part(lambda array: array), fill=fill)
        rows = pack_rows // self.blocks

        def of_block(index):
            firsts = self.first_rows(index, rows)
            return part(
                lambda array: jnp.concatenate(
                    [rows_at(array, first, rows) for first in firsts], axis=0
                )
            )

        return self.collect(of_block, fill=fill)


def sum_over_all(array, axes):
    for axis in axes:
        size = lax.axis_size(axis)
        step = 1
        while step < size:
            array = array + lax.ppermute(array, axis, [(k, k ^ step) for k in range(size)])
            step *= 2
    return array


def attend_kernel(query_ref, key_ref, value_ref, row_ids_ref, col_ids_ref, out_ref):
    scores = mat_times_t(query_ref[...], key_ref[...]) * HEAD ** (-0.5)
    mask = row_ids_ref[...] == col_ids_ref[...]
    scores = jnp.where(mask, scores, masked_score)
    top = jnp.max(scores, axis=-1, keepdims=True)
    weights = jnp.exp(scores - top)
    total = jnp.sum(weights, axis=-1, keepdims=True)
    probs = (weights * (1.0 / total)).astype(low)
    out_ref[...] = mat_times(probs, value_ref[...]).astype(low)


def query_rows_for(rows):
    return 256 if rows <= 2048 else 64


def attend(heads, row_ids, col_ids):
    rows = heads.shape[0]
    width = query_rows_for(rows)
    return pl.pallas_call(
        attend_kernel,
        out_shape=jax.ShapeDtypeStruct((rows, LANES), low),
        grid=(rows // width,),
        in_specs=[
            pl.BlockSpec((width, LANES), lambda i: (i, 0)),
            pl.BlockSpec((rows, LANES), lambda i: (0, 1)),
            pl.BlockSpec((rows, LANES), lambda i: (0, 2)),
            pl.BlockSpec((width, 1), lambda i: (i, 0)),
            pl.BlockSpec((1, rows), lambda i: (0, 0)),
        ],
        out_specs=pl.BlockSpec((width, LANES), lambda i: (i, 0)),
        compiler_params=pltpu.CompilerParams(vmem_limit_bytes=vmem_bytes),
        name="vision_attend",
    )(heads, heads, heads, row_ids, col_ids)


def attend_back_kernel(
    query_ref, key_ref, value_ref, grad_ref, row_ids_ref, col_ids_ref,
    query_grad_ref, key_grad_ref, value_grad_ref, key_sum, value_sum,
):
    step = pl.program_id(0)

    @pl.when(step == 0)
    def _():
        key_sum[...] = jnp.zeros_like(key_sum)
        value_sum[...] = jnp.zeros_like(value_sum)

    queries = query_ref[...]
    grads = grad_ref[...]
    scores = mat_times_t(key_ref[...], queries) * HEAD ** (-0.5)
    mask = row_ids_ref[...] == col_ids_ref[...]
    scores = jnp.where(mask, scores, masked_score)
    top = jnp.max(scores, axis=0, keepdims=True)
    weights = jnp.exp(scores - top)
    total = jnp.sum(weights, axis=0, keepdims=True)
    probs = weights * (1.0 / total)
    dprob = mat_times_t(value_ref[...], grads)
    delta = jnp.sum(probs * dprob, axis=0, keepdims=True)
    score_grad = (probs * (dprob - delta)).astype(low)
    key_sum[...] += mat_times(score_grad, queries)
    value_sum[...] += mat_times(probs.astype(low), grads)
    query_grad_ref[...] = (outer_sum(score_grad, key_ref[...]) * HEAD ** (-0.5)).astype(low)

    @pl.when(step == pl.num_programs(0) - 1)
    def _():
        key_grad_ref[...] = (key_sum[...] * HEAD ** (-0.5)).astype(low)
        value_grad_ref[...] = value_sum[...].astype(low)


def attend_back(heads, grads, row_ids, col_ids):
    rows = heads.shape[0]
    width = query_rows_for(rows)
    return pl.pallas_call(
        attend_back_kernel,
        out_shape=[jax.ShapeDtypeStruct((rows, LANES), low)] * 3,
        grid=(rows // width,),
        in_specs=[
            pl.BlockSpec((width, LANES), lambda i: (i, 0)),
            pl.BlockSpec((rows, LANES), lambda i: (0, 1)),
            pl.BlockSpec((rows, LANES), lambda i: (0, 2)),
            pl.BlockSpec((width, LANES), lambda i: (i, 0)),
            pl.BlockSpec((rows, 1), lambda i: (0, 0)),
            pl.BlockSpec((1, width), lambda i: (0, i)) if width % LANES == 0
            else pl.BlockSpec((None, 1, width), lambda i: (i, 0, 0)),
        ],
        out_specs=[
            pl.BlockSpec((width, LANES), lambda i: (i, 0)),
            pl.BlockSpec((rows, LANES), lambda i: (0, 0)),
            pl.BlockSpec((rows, LANES), lambda i: (0, 0)),
        ],
        scratch_shapes=[pltpu.VMEM((rows, LANES), wide)] * 2,
        compiler_params=pltpu.CompilerParams(vmem_limit_bytes=vmem_bytes),
        name="vision_attend_back",
    )(
        heads, heads, heads, grads, row_ids,
        col_ids if width % LANES == 0 else col_ids.reshape(rows // width, 1, width),
    )


def image_probs(scores, self_scores, mask):
    scores = jnp.where(mask, scores, masked_score)
    top = jnp.maximum(
        jnp.max(scores, axis=-1, keepdims=True), jnp.max(self_scores, axis=-1, keepdims=True)
    )
    weights = jnp.where(mask, jnp.exp(scores - top), 0.0)
    self_weights = jnp.exp(self_scores - top)
    total = jnp.sum(weights, axis=-1, keepdims=True) + jnp.sum(
        self_weights, axis=-1, keepdims=True
    )
    scale = 1.0 / total
    return weights * scale, self_weights * scale


def resample_kernel(
    query_ref, key_ref, value_ref, self_key_ref, self_value_ref, ids_ref, out_ref, *, images
):
    queries = query_ref[...]
    scores = mat_times_t(queries, key_ref[...]) * P_HEAD ** (-0.5)
    self_scores = mat_times_t(queries, self_key_ref[...]) * P_HEAD ** (-0.5)
    for image in range(images):
        probs, self_probs = image_probs(scores, self_scores, ids_ref[...] == image)
        mixed = mat_times(probs.astype(low), value_ref[...])
        mixed += mat_times(self_probs.astype(low), self_value_ref[...])
        out_ref[pl.ds(image * LATENTS, LATENTS), :] = mixed.astype(low)


def resample(queries, keys, values, self_keys, self_values, ids, images):
    return pl.pallas_call(
        functools.partial(resample_kernel, images=images),
        out_shape=jax.ShapeDtypeStruct((images * LATENTS, LANES), low),
        compiler_params=pltpu.CompilerParams(vmem_limit_bytes=vmem_bytes),
        name="resampler_attend",
    )(queries, keys, values, self_keys, self_values, ids)


def resample_back_kernel(
    query_ref, key_ref, value_ref, self_key_ref, self_value_ref, ids_ref, grad_ref,
    query_grad_ref, key_grad_ref, value_grad_ref, self_key_grad_ref, self_value_grad_ref,
    *, images,
):
    queries = query_ref[...]
    scale = P_HEAD ** (-0.5)
    scores = mat_times_t(queries, key_ref[...]) * scale
    self_scores = mat_times_t(queries, self_key_ref[...]) * scale
    for image in range(images):
        probs, self_probs = image_probs(scores, self_scores, ids_ref[...] == image)
        grads = grad_ref[pl.ds(image * LATENTS, LATENTS), :]
        dprob = mat_times_t(grads, value_ref[...])
        self_dprob = mat_times_t(grads, self_value_ref[...])
        delta = jnp.sum(probs * dprob, axis=-1, keepdims=True) + jnp.sum(
            self_probs * self_dprob, axis=-1, keepdims=True
        )
        score_grad = (probs * (dprob - delta)).astype(low)
        self_score_grad = (self_probs * (self_dprob - delta)).astype(low)
        terms = (
            mat_times(score_grad, key_ref[...]) + mat_times(self_score_grad, self_key_ref[...]),
            outer_sum(score_grad, queries),
            outer_sum(probs.astype(low), grads),
            outer_sum(self_score_grad, queries),
            outer_sum(self_probs.astype(low), grads),
        )
        refs = (
            query_grad_ref, key_grad_ref, value_grad_ref, self_key_grad_ref, self_value_grad_ref
        )
        for ref, term in zip(refs, terms):
            if image == 0:
                ref[...] = term
            else:
                ref[...] += term


def resample_back(queries, keys, values, self_keys, self_values, ids, grads, images):
    rows = keys.shape[0]
    shapes = [(LATENTS, LANES), (rows, LANES), (rows, LANES), (LATENTS, LANES), (LATENTS, LANES)]
    return pl.pallas_call(
        functools.partial(resample_back_kernel, images=images),
        out_shape=[jax.ShapeDtypeStruct(shape, wide) for shape in shapes],
        compiler_params=pltpu.CompilerParams(vmem_limit_bytes=vmem_bytes),
        name="resampler_attend_back",
    )(queries, keys, values, self_keys, self_values, ids, grads)


def lane_pad(array):
    gap = [(0, 0)] * (array.ndim - 1) + [(0, LANES - array.shape[-1])]
    return jnp.pad(array, gap)


def context_back_kernel(
    order_ref, context_ref, grad_ref, weight_ref, gain_ref, out_ref, scale_ref, gain_grad_ref
):
    step = pl.program_id(0)
    grads = mat_times(grad_ref[...], weight_ref[...])
    values = context_ref[...].astype(wide)
    scale = lax.rsqrt(jnp.mean(values * values, axis=-1, keepdims=True) + norm_eps)
    unit = values * scale
    scaled = grads * gain_ref[...]
    share = jnp.mean(scaled * unit, axis=-1, keepdims=True)
    out_ref[...] = (scale * (scaled - unit * share)).astype(low)
    scale_ref[...] = scale
    gain_grad = jnp.sum(grads * unit, axis=0, keepdims=True)

    @pl.when(step == 0)
    def _():
        gain_grad_ref[...] = gain_grad

    @pl.when(step > 0)
    def _():
        gain_grad_ref[...] += gain_grad


def context_back(order, context, grads, weight, gain):
    pack_rows, model = context.shape
    rows = pack_rows // order.shape[0]
    width = grads.shape[1]
    return pl.pallas_call(
        context_back_kernel,
        out_shape=[
            jax.ShapeDtypeStruct((pack_rows, model), low),
            jax.ShapeDtypeStruct((pack_rows, 1), wide),
            jax.ShapeDtypeStruct((1, model), wide),
        ],
        grid_spec=pltpu.PrefetchScalarGridSpec(
            num_scalar_prefetch=1,
            grid=(order.shape[0],),
            in_specs=[
                pl.BlockSpec((rows, model), lambda i, order: (order[i], 0)),
                pl.BlockSpec((rows, width), lambda i, order: (i, 0)),
                pl.BlockSpec((width, model), lambda i, order: (0, 0)),
                pl.BlockSpec((1, model), lambda i, order: (0, 0)),
            ],
            out_specs=[
                pl.BlockSpec((rows, model), lambda i, order: (i, 0)),
                pl.BlockSpec((rows, 1), lambda i, order: (i, 0)),
                pl.BlockSpec((1, model), lambda i, order: (0, 0)),
            ],
        ),
        compiler_params=pltpu.CompilerParams(vmem_limit_bytes=vmem_bytes),
        name="context_back",
    )(order, context, grads, weight, gain[None, :])


def on_device(
    tokens, segment_ids, ln1_gain, ln1_bias, qkv_weight, q_bias, v_bias, out_weight, out_bias,
    ln2_gain, ln2_bias, fc1_weight, fc1_bias, fc2_weight, fc2_bias, bridge_gate, bridge_up,
    bridge_down, context_gain, latents, latent_gain, query_weight, key_weight, value_weight,
    mixer_weight, post_gain, latent_gate, latent_up, latent_down, cotangent,
):
    blocks = lax.axis_size("blk")
    planes = lax.axis_size("grp")
    me = lax.axis_index("blk")
    plane = lax.axis_index("grp")
    rows, features = tokens.shape
    pack_rows = rows * blocks
    hidden_units = fc1_weight.shape[1]
    unit_share = -(-hidden_units // blocks)
    model = latents.shape[1]
    model_share = query_weight.shape[0]
    lat_rows = cotangent.shape[0]
    lat_own = lat_rows // blocks
    images = lat_rows // LATENTS
    copies = blocks // HEADS
    head = me // copies
    part = me % copies
    kv_head = head // (P_HEADS // P_KV)
    walk = Walk(blocks)

    def other_plane(array, step=1):
        return lax.ppermute(array, "grp", [(k, (k + step) % planes) for k in range(planes)])

    def shared_from_other_plane(array):
        core = me % 2
        half = array.shape[0] // 2
        own = other_plane(rows_at(array, core * half, half))
        sibling = walk.swap(own)
        return jnp.concatenate(
            [jnp.where(core == 0, own, sibling), jnp.where(core == 0, sibling, own)], axis=0
        )

    def in_plane_order(array, other):
        return jnp.concatenate(
            [jnp.where(plane == 0, array, other), jnp.where(plane == 0, other, array)], axis=0
        )

    def plane_sum(mine, others, last):
        others = lax.optimization_barrier((others, last))[0]
        return functools.reduce(
            lambda total, other: total + other.astype(wide), others, mine.astype(wide)
        )

    def joined(blocks):
        return blocks[0] if len(blocks) == 1 else jnp.concatenate(blocks, axis=0)

    def to_columns(weight):
        padded = jnp.pad(weight, ((0, 0), (0, unit_share * blocks - weight.shape[1])))
        return jnp.transpose(padded.reshape(weight.shape[0], blocks, unit_share), (1, 0, 2))

    def share_rows(matrix):
        width = matrix.shape[0] // planes
        total = None
        for step in range(planes):
            piece = rows_at(matrix, (plane + step) % planes * width, width).astype(low)
            pairs = [
                (k * blocks + j, planes * j + (k + step) % planes)
                for k in range(planes)
                for j in range(blocks)
            ]
            arrived = lax.ppermute(piece, ("grp", "blk"), pairs).astype(wide)
            total = arrived if total is None else total + arrived
        return total

    def column_pieces(matrix):
        width = matrix.shape[0] // (planes * blocks)
        return jnp.transpose(matrix.reshape(planes, blocks, width, -1), (1, 0, 2, 3))

    def plane_share(arrived):
        arrived = arrived.reshape((blocks, planes, -1) + arrived.shape[2:])
        total = lax.dynamic_index_in_dim(arrived, plane, 1, keepdims=False).astype(wide)
        for step in range(1, planes):
            piece = lax.dynamic_index_in_dim(
                arrived, (plane + step) % planes, 1, keepdims=False
            )
            total = total + other_plane(piece, step).astype(wide)
        return total

    made = {}

    def filler(names, make):
        def work(sent):
            results = make(sent)
            made.update(zip(names, results))
            return tuple(results)

        return work

    def nothing(_):
        return ()

    head_pieces = lane_pad(qkv_weight.reshape(-1, 3, HEADS, HEAD))
    head_pieces = jnp.transpose(head_pieces, (2, 0, 1, 3)).reshape(HEADS, -1, 3 * LANES)
    id_rows = jnp.pad(segment_ids.astype(low)[None, None, :], ((0, 0), (0, 7), (0, 0)))
    id_rows = jnp.tile(id_rows, (blocks, 1, 3 * LANES // rows + 1))[..., : 3 * LANES]
    head_pieces = jnp.concatenate(
        [jnp.repeat(head_pieces, copies, axis=0), id_rows], axis=1
    )

    def bring_heads(sent):
        arrived = swap_pieces(after(head_pieces, sent)).reshape(head_pieces.shape)
        weight = arrived[:, : arrived.shape[1] - 8].reshape(-1, 3 * LANES)
        ids = arrived[:, arrived.shape[1] - 8, :rows].reshape(-1)
        return weight, ids.astype(jnp.int32)

    fc1_bias_own = rows_at(
        jnp.pad(fc1_bias, (0, unit_share * blocks - hidden_units)), me * unit_share, unit_share
    )
    head_bias = jnp.concatenate(
        [
            lane_pad(rows_at(q_bias, head * HEAD, HEAD)),
            jnp.zeros((LANES,), wide),
            lane_pad(rows_at(v_bias, head * HEAD, HEAD)),
        ]
    )

    inputs = tokens.astype(wide)
    normed, first_norm_back = jax.vjp(layer_norm, inputs, ln1_gain, ln1_bias)

    def make_units(sent):
        both = [to_columns(after(one, sent)) for one in (fc1_weight, fc2_weight)]
        return (jnp.concatenate(both, axis=2),)

    first_rows = walk.gather(
        normed.astype(low),
        [
            filler(("unit_pieces",), make_units),
            filler(("head_weight", "all_ids"), bring_heads),
        ],
    )
    head_weight, all_ids = made["head_weight"], made["all_ids"]
    cotangent = after(cotangent, first_rows)
    out_full = gather(after(out_weight, first_rows))
    pair_half = jnp.where(plane == 0, key_weight, value_weight)
    pair_half = gather(after(pair_half, out_full))
    row_ids = all_ids[:, None]
    col_ids = all_ids[None, :]
    heads = (mat_times(first_rows, head_weight) + head_bias).astype(low)
    unit_weights = swap_pieces(made["unit_pieces"])
    fc1_own = unit_weights[:, :unit_share]
    fc2_own = unit_weights[:, unit_share:]
    attended_head = after(attend(heads, row_ids, col_ids), unit_weights)
    attended_pieces = swap_pieces(attended_head[:, :HEAD].reshape(blocks, rows, HEAD))
    attended_pieces = attended_pieces.reshape(blocks, rows, HEAD)[::copies]
    attended = jnp.transpose(attended_pieces, (1, 0, 2)).reshape(rows, features)
    hidden_state = inputs + mat_times(attended, out_full) + out_bias

    second, second_norm_back = jax.vjp(layer_norm, hidden_state, ln2_gain, ln2_bias)
    cotangent_other = shared_from_other_plane(cotangent)

    def use_cotangent(_):
        return (cotangent_other,)

    second_blocks = walk.spread(second.astype(low), [nothing, nothing, use_cotangent])
    pre_blocks = [mat_times(block, fc1_own) + fc1_bias_own for block in second_blocks]
    act_blocks = [smooth_gate(pre).astype(low) for pre in pre_blocks]
    encoded = walk.collect(lambda i: mat_times_t(act_blocks[i], fc2_own))
    encoded = after(hidden_state + encoded + fc2_bias, pair_half)

    bridge_blocks = walk.spread(encoded.astype(low))
    gate_blocks = [mat_times(block, bridge_gate) for block in bridge_blocks]
    up_blocks = [mat_times(block, bridge_up) for block in bridge_blocks]
    hidden_blocks = [swiglu(gate, up).astype(low) for gate, up in zip(gate_blocks, up_blocks)]
    latent_normed, latent_norm_back = jax.vjp(rms_norm, latents.astype(wide), latent_gain)
    latent_in = latent_normed.astype(low)
    latent_in_own = rows_at(latent_in, me * model_share, model_share, 1)
    query_width = P_HEADS * P_HEAD
    pair_width = P_KV * P_HEAD


    def heads_of(matrix, count):
        split = lane_pad(matrix.reshape(LATENTS, count, P_HEAD))
        split = jnp.transpose(split, (1, 0, 2))
        return jnp.repeat(split, blocks // count, axis=0)

    latent_pieces = jnp.concatenate(
        [
            heads_of(mat_times(latent_in_own, query_weight), P_HEADS),
            heads_of(mat_times(latent_in_own, key_weight), P_KV),
            heads_of(mat_times(latent_in_own, value_weight), P_KV),
        ],
        axis=2,
    ).astype(low)
    mixer_pieces = jnp.transpose(mixer_weight.reshape(-1, blocks, model // blocks), (1, 0, 2))

    def bring_latents(sent):
        arrived = swap_pieces(after(latent_pieces, sent)).reshape(blocks, LATENTS, 3 * LANES)
        return (jnp.sum(arrived.astype(wide), axis=0).astype(low),)

    def bring_mixer(sent):
        return (swap_pieces(after(mixer_pieces, sent)),)

    def bring_pairs(sent):
        halves = [after(one, sent) for one in (pair_half, other_half)]
        key_full = jnp.where(plane == 0, halves[0], halves[1])
        value_full = jnp.where(plane == 0, halves[1], halves[0])
        pair_weight = jnp.concatenate([key_full, value_full], axis=1)
        return pair_weight, jnp.transpose(pair_weight)

    other_half = other_plane(pair_half)
    context = walk.collect(
        lambda i: mat_times(hidden_blocks[i], bridge_down),
        2,
        [
            filler(("latent_proj",), bring_latents),
            filler(("mixer_own",), bring_mixer),
            filler(("pair_weight", "pair_turned"), bring_pairs),
        ],
    )
    latent_proj, mixer_own = made["latent_proj"], made["mixer_own"]
    pair_weight, pair_turned = made["pair_weight"], made["pair_turned"]
    latent_query = latent_proj[:, :LANES]
    latent_key = latent_proj[:, LANES : 2 * LANES]
    latent_value = latent_proj[:, 2 * LANES :]


    context_in = rms_norm(context, context_gain).astype(low)
    patch_pairs = walk.gather(mat_times(context_in, pair_weight).astype(low))
    def head_of(matrix, first, index):
        return lane_pad(rows_at(matrix, first + index * P_HEAD, P_HEAD, 1))

    patch_key = head_of(patch_pairs, 0, kv_head)
    patch_value = head_of(patch_pairs, pair_width, kv_head)
    attended_latent_head = resample(
        latent_query, patch_key, patch_value, latent_key, latent_value, col_ids, images
    )[:, :P_HEAD]
    attended_latent = walk.gather(attended_latent_head).reshape(blocks, lat_rows, P_HEAD)[::copies]
    attended_latent = jnp.transpose(attended_latent, (1, 0, 2)).reshape(lat_rows, query_width)
    mixed = walk.gather(mat_times(attended_latent, mixer_own).astype(low))
    context_rows = gather(after(context.astype(low), mixed))
    mixed = jnp.transpose(mixed.reshape(blocks, lat_rows, -1), (1, 0, 2)).reshape(lat_rows, model)
    latent_state = jnp.tile(latents.astype(wide), (images, 1)) + mixed.astype(wide)

    post_in = rms_norm(latent_state, post_gain).astype(low)
    latent_gate_pre = mat_times(post_in, latent_gate)
    latent_up_pre = mat_times(post_in, latent_up)
    latent_hidden = swiglu(latent_gate_pre, latent_up_pre).astype(low)
    own_start = me * lat_own
    state_own = rows_at(latent_state, own_start, lat_own)
    latent_gate_grad, latent_up_grad = swiglu_back(
        latent_gate_pre, latent_up_pre, mat_times_t(cotangent, latent_down)
    )
    latent_gate_low = latent_gate_grad.astype(low)
    latent_up_low = latent_up_grad.astype(low)
    lat_units = latent_hidden.shape[1]
    units = jnp.concatenate([latent_gate_low, latent_up_low, latent_hidden], axis=1)
    post_part = mat_times_t(latent_gate_low, latent_gate) + mat_times_t(latent_up_low, latent_up)
    post_part = post_part.astype(low)
    post_grad = walk.collect_rows(lambda take: take(post_part), lat_rows)
    _, post_norm_back = jax.vjp(rms_norm, state_own, post_gain)
    state_norm_grad, post_gain_part = post_norm_back(post_grad)
    state_grad = rows_at(cotangent, own_start, lat_own).astype(wide) + state_norm_grad
    state_low = walk.gather(state_grad.astype(low))
    resid = jnp.sum(state_low.astype(wide).reshape(images, LATENTS, model), axis=0)
    resid_low = resid.astype(low)

    latent_att_grad = mat_times_t(state_low, mixer_weight).astype(low)
    if copies > 1:
        latent_att_grad = gather(latent_att_grad).reshape(blocks, lat_rows, -1)
        latent_att_grad = jnp.transpose(latent_att_grad, (1, 0, 2)).reshape(lat_rows, query_width)
        latent_att_grad = rows_at(latent_att_grad, head * P_HEAD, P_HEAD, 1)
    query_part, patch_key_part, patch_value_part, latent_key_part, latent_value_part = (
        resample_back(
            latent_query, patch_key, patch_value, latent_key, latent_value, col_ids,
            lane_pad(latent_att_grad), images,
        )
    )
    scale_latent = P_HEAD ** (-0.5)
    latent_table = jnp.concatenate(
        [query_part * scale_latent, latent_key_part * scale_latent, latent_value_part], axis=1
    )
    latent_total = latent_table
    for step in range(1, planes):
        latent_total = latent_total + other_plane(latent_table, step)
    patch_part = jnp.concatenate(
        [patch_key_part[:, :P_HEAD] * scale_latent, patch_value_part[:, :P_HEAD]], axis=1
    ).astype(low)
    patch_part = swap_pieces(patch_part.reshape(blocks, rows, 2 * P_HEAD))
    units_other = other_plane(after(units, latent_total))
    post_other = shared_from_other_plane(after(post_in, latent_total))
    patch_part = after(patch_part, context_rows)
    patch_part = patch_part.reshape(blocks, rows, 2, P_HEAD)[::copies].astype(wide)
    patch_grad = jnp.sum(
        patch_part.reshape(P_KV, P_HEADS // P_KV, rows, 2, P_HEAD), axis=1
    )
    patch_grad = jnp.transpose(patch_grad, (1, 2, 0, 3)).reshape(rows, 2 * pair_width).astype(low)
    latent_rows = gather(jnp.pad(latent_total.astype(low), ((0, 0), (0, LANES))))
    patch_grad_rows = joined(walk.spread(patch_grad))
    context_low, context_scale, context_gain_part = context_back(
        walk.device_order(), context_rows, patch_grad_rows, pair_turned, context_gain
    )
    context_gain_part = jnp.where(me == 0, context_gain_part[0], 0.0)

    size = bridge_blocks[0].shape[0]
    context_blocks = [
        context_low[k * size : (k + 1) * size] for k in range(len(bridge_blocks))
    ]
    gate_low, up_low = (
        one.astype(low)
        for one in swiglu_back(
            joined(gate_blocks), joined(up_blocks), mat_times_t(context_low, bridge_down)
        )
    )
    bridge_rows = joined(bridge_blocks)
    hidden_joined = joined(hidden_blocks)

    def encoded_terms(index):
        span = slice(index * size, (index + 1) * size)
        return mat_times_t(gate_low[span], bridge_gate) + mat_times_t(up_low[span], bridge_up)

    def make_down(sent):
        return (outer_sum(hidden_joined, after(context_low, sent)).astype(low),)

    def make_gate(sent):
        return (outer_sum(bridge_rows, after(gate_low, sent)).astype(low),)

    def make_up(sent):
        grad = outer_sum(bridge_rows, after(up_low, sent)).astype(low)
        return grad, jnp.concatenate([made["gate"], grad], axis=1)

    encoded_grad = walk.collect(
        encoded_terms,
        fill=[filler(("down",), make_down), filler(("gate",), make_gate), filler(("up", "gate_up"), make_up)],
    )
    part_bridge_down = made["down"]
    down_others = [other_plane(part_bridge_down, step) for step in range(1, planes)]
    part_bridge_gate, part_bridge_up = made["gate"], made["up"]
    pair_others = [other_plane(made["gate_up"], step) for step in range(1, planes)]

    def rows_of_both(sent, array, other):
        return in_plane_order(after(array, sent), after(other, sent))

    def make_latent_gate(sent):
        made["units"] = rows_of_both(sent, units, units_other)
        made["post"] = rows_of_both(sent, post_in, post_other)
        return (outer_sum(made["post"], made["units"][:, :lat_units]),)

    def make_latent_up(sent):
        both = after(made["units"], sent)
        return (outer_sum(made["post"], both[:, lat_units : 2 * lat_units]),)

    def make_latent_down(sent):
        both = rows_of_both(sent, cotangent, cotangent_other)
        return (outer_sum(made["units"][:, 2 * lat_units :], both),)

    encoded_blocks = walk.spread(
        encoded_grad.astype(low),
        [
            filler(("latent_gate",), make_latent_gate),
            filler(("latent_up",), make_latent_up),
            filler(("latent_down",), make_latent_down),
        ],
    )
    grad_latent_gate, grad_latent_up = made["latent_gate"], made["latent_up"]
    grad_latent_down = made["latent_down"]
    grad_fc2_bias = jnp.sum(encoded_grad, axis=0)
    pre_grad_blocks = [
        jax.vjp(smooth_gate, pre)[1](mat_times(block, fc2_own))[0].astype(low)
        for pre, block in zip(pre_blocks, encoded_blocks)
    ]

    def make_pair(sent):
        columns = walk.in_own_order(
            rows_at(after(context_rows, sent), me * model_share, model_share, 1)
        )
        columns = columns.astype(wide) * context_scale
        columns = columns * rows_at(context_gain, me * model_share, model_share)
        return (outer_sum(columns.astype(low), patch_grad_rows),)

    def make_fc1(sent):
        return (outer_sum(after(joined(second_blocks), sent), joined(pre_grad_blocks)).astype(low),)

    def make_fc2(sent):
        grad = outer_sum(after(joined(encoded_blocks), sent), joined(act_blocks)).astype(low)
        return (column_pieces(jnp.concatenate([made["fc1"], grad], axis=1)),)

    second_grad = walk.collect(
        lambda i: mat_times_t(pre_grad_blocks[i], fc1_own),
        fill=[
            filler(("pair",), make_pair),
            filler(("fc1",), make_fc1),
            filler(("unit_pieces_back",), make_fc2),
        ],
    )
    pre_grad = joined(pre_grad_blocks)
    grad_fc1_bias = jnp.sum(pre_grad.astype(wide), axis=0)
    hidden_norm_grad, grad_ln2_gain, grad_ln2_bias = second_norm_back(second_grad)
    hidden_grad = encoded_grad + hidden_norm_grad
    grad_out_bias = jnp.sum(hidden_grad, axis=0)
    hidden_low = hidden_grad.astype(low)


    def make_tables(sent):
        latent_tables = after(latent_rows, sent)[:, : 3 * LANES]
        latent_tables = latent_tables.reshape(blocks, LATENTS, 3, LANES)
        latent_tables = latent_tables[::copies, :, :, :P_HEAD]
        query_grad = jnp.transpose(latent_tables[:, :, 0], (1, 0, 2)).reshape(LATENTS, query_width)
        pair_grad = jnp.sum(
            latent_tables[:, :, 1:]
            .astype(wide)
            .reshape(P_KV, P_HEADS // P_KV, LATENTS, 2, P_HEAD),
            axis=1,
        )
        pair_grad = jnp.transpose(pair_grad, (1, 2, 0, 3)).reshape(LATENTS, 2 * pair_width)
        pair_grad = pair_grad.astype(low)
        return query_grad, pair_grad

    def make_latent_in(sent):
        query_grad, pair_grad = after(made["query_grad"], sent), made["pair_grad"]
        latent_in_grad = (
            mat_times_t(query_grad, query_weight)
            + mat_times_t(pair_grad[:, :pair_width], key_weight)
            + mat_times_t(pair_grad[:, pair_width:], value_weight)
        )
        made["latent_in_grad"] = gather(latent_in_grad)
        made["latents"] = scatter_sum(mat_times(after(latent_hidden, sent), latent_down))
        return (latent_in_grad,)

    def bring_units(sent):
        made["unit_grads"] = swap_pieces(after(made["unit_pieces_back"], sent))
        return ()

    hidden_rows = walk.gather(
        hidden_low,
        [
            bring_units,
            filler(("query_grad", "pair_grad"), make_tables),
        ],
    )
    out_own = rows_at(out_full, head * HEAD, HEAD) if copies > 1 else out_weight
    attended_grad = lane_pad(mat_times_t(hidden_rows, out_own).astype(low))
    attended_grad = after(attended_grad, made["unit_grads"])
    query_low, key_low, value_low = attend_back(heads, attended_grad, row_ids, col_ids)
    head_grad = jnp.concatenate([query_low, key_low, value_low], axis=1)

    def make_heads(sent):
        grad = outer_sum(after(first_rows, sent), head_grad).astype(low)
        return (column_pieces(grad),)

    def note_late(sent):
        made["late"] = sent
        return ()

    bridge_units = bridge_gate.shape[1]
    first_weight = head_weight
    if copies > 1:
        first_weight = jnp.where(part == 0, head_weight, jnp.zeros((), low))
    first_grad = walk.collect_rows(
        lambda take: mat_times_t(take(head_grad), first_weight),
        pack_rows,
        [
            filler(("heads",), make_heads),
            filler(("latent_part",), make_latent_in),
            nothing,
            note_late,
        ],
    )
    input_norm_grad, grad_ln1_gain, grad_ln1_bias = first_norm_back(first_grad)
    grad_tokens = hidden_grad + input_norm_grad

    resid_others = [
        other_plane(after(resid_low, first_grad), step) for step in range(1, planes)
    ]
    mixer_width = mixer_weight.shape[0]
    grad_mixer = share_rows(
        outer_sum(
            rows_at(attended_latent_head, part * mixer_width, mixer_width, 1),
            after(state_low, first_grad),
        )
    )
    grad_pair = share_rows(after(made["pair"], first_grad))
    out_width = out_weight.shape[0]
    grad_out = outer_sum(rows_at(attended_head, part * out_width, out_width, 1), hidden_rows)
    grad_out = share_rows(after(grad_out, first_grad))
    units = plane_share(after(made["unit_grads"], first_grad))
    units = jnp.transpose(
        units.reshape(blocks, units.shape[1], 2, unit_share), (2, 1, 0, 3)
    ).reshape(2, units.shape[1], -1)[:, :, :hidden_units]
    grad_qkv = plane_share(swap_pieces(made["heads"]))[::copies]
    grad_qkv = grad_qkv.reshape(HEADS, grad_qkv.shape[1], 3, LANES)[..., :HEAD]
    grad_qkv = jnp.transpose(grad_qkv, (1, 2, 0, 3)).reshape(-1, 3 * features)
    once = (part == 0).astype(wide)

    def spread(width, piece, first):
        return lax.dynamic_update_slice_in_dim(jnp.zeros((width,), wide), piece, first, 0)

    def packed(arrays):
        flat = jnp.concatenate([array.reshape(-1) for array in arrays])
        gap = -flat.shape[0] % (8 * LANES)
        return jnp.pad(flat, (0, gap)).reshape(-1, LANES)

    def unpacked(table, arrays):
        flat = table.reshape(-1)
        first = 0
        pieces = []
        for array in arrays:
            pieces.append(flat[first : first + array.size].reshape(array.shape))
            first += array.size
        return pieces

    query_bias_part = jnp.sum(query_low[:, :HEAD].astype(wide), axis=0) * once
    value_bias_part = jnp.sum(value_low[:, :HEAD].astype(wide), axis=0) * once
    small_terms = (
        grad_ln1_gain,
        grad_ln1_bias,
        spread(features, query_bias_part, head * HEAD),
        spread(features, value_bias_part, head * HEAD),
        grad_out_bias,
        grad_ln2_gain,
        grad_ln2_bias,
        spread(unit_share * blocks, grad_fc1_bias, me * unit_share),
        grad_fc2_bias,
        context_gain_part,
        post_gain_part,
    )
    small = unpacked(sum_over_all(packed(small_terms), ("grp", "blk")), small_terms)
    bridge_units = bridge_gate.shape[1]
    grad_bridge_down = plane_sum(part_bridge_down, down_others, made["late"])
    pair_others = [after(other, first_grad) for other in pair_others]
    grad_bridge_gate = plane_sum(
        part_bridge_gate, [other[:, :bridge_units] for other in pair_others], first_grad
    )
    grad_bridge_up = plane_sum(
        part_bridge_up, [other[:, bridge_units:] for other in pair_others], first_grad
    )
    latents_out = (state_own + after(made["latents"], first_grad)).astype(low)

    query_grad, pair_grad = made["query_grad"], made["pair_grad"]
    latent_in_grad = after(made["latent_in_grad"], first_grad)
    latent_in_grad = latent_in_grad.reshape(blocks, LATENTS, model_share)
    latent_in_grad = jnp.transpose(latent_in_grad, (1, 0, 2)).reshape(LATENTS, model)
    latent_grad, grad_latent_gain = latent_norm_back(latent_in_grad)
    grad_latents = latent_grad + plane_sum(resid_low, resid_others, first_grad)
    share = model // (planes * blocks)
    latent_in_share = rows_at(latent_in, (plane * blocks + me) * share, share, 1)
    grad_query = outer_sum(latent_in_share, query_grad)
    grad_pair = grad_pair + outer_sum(latent_in_share, pair_grad)
    return (
        latents_out,
        grad_tokens,
        small[0],
        small[1],
        grad_qkv,
        small[2],
        small[3],
        grad_out,
        small[4],
        small[5],
        small[6],
        units[0],
        small[7][:hidden_units],
        units[1],
        small[8],
        grad_bridge_gate,
        grad_bridge_up,
        grad_bridge_down,
        small[9],
        grad_latents,
        grad_latent_gain,
        grad_query,
        grad_pair[:, :pair_width],
        grad_pair[:, pair_width:],
        grad_mixer,
        small[10],
        grad_latent_gate,
        grad_latent_up,
        grad_latent_down,
    )


def solution(mesh):
    in_specs = (
        P(("grp", "blk"), None),
        P(("grp", "blk")),
        P(),
        P(),
        P("blk", None),
        P(),
        P(),
        P("blk", None),
        P(),
        P(),
        P(),
        P("blk", None),
        P(),
        P("blk", None),
        P(),
        P(None, "blk"),
        P(None, "blk"),
        P("blk", None),
        P(),
        P(),
        P(),
        P("blk", None),
        P("blk", None),
        P("blk", None),
        P("blk", None),
        P(),
        P(None, "blk"),
        P(None, "blk"),
        P("blk", None),
        P("grp", None),
    )
    out_specs = (
        P(("grp", "blk"), None),
        P(("grp", "blk"), None),
        P(),
        P(),
        P(("grp", "blk"), None),
        P(),
        P(),
        P(("grp", "blk"), None),
        P(),
        P(),
        P(),
        P(("grp", "blk"), None),
        P(),
        P(("grp", "blk"), None),
        P(),
        P(None, "blk"),
        P(None, "blk"),
        P("blk", None),
        P(),
        P(),
        P(),
        P(("grp", "blk"), None),
        P(("grp", "blk"), None),
        P(("grp", "blk"), None),
        P(("grp", "blk"), None),
        P(),
        P(None, "blk"),
        P(None, "blk"),
        P("blk", None),
    )
    return jax.shard_map(
        on_device, mesh=mesh, in_specs=in_specs, out_specs=out_specs, check_vma=False
    )
```
